32 devices in a mesh: rows: 8 (over y, x, core), ch: 4 (over z).
Axes of the slice: x: 2, y: 2, z: 4, core: 2. Of those that a mesh axis runs over, the one named last changes fastest.
Arguments:
- frames: bfloat16 [128, 1024, 512], P('rows', None, 'ch'), may hold values from -6 to 6
- style_vector: bfloat16 [128, 4, 128], P('rows'), may hold values from -5 to 5
- segment_ids: int32 [128, 1024], P('rows'), may hold values from 0 to 3, as said below
- padding: int32 [128, 1024], P('rows'), may hold values from 0 to 1, as said below
- fc1_weight: bfloat16 [2, 128, 512], P(None, None, 'ch'), may hold values from -0.375 to 0.375
- fc1_bias: bfloat16 [2, 512], P(None, 'ch'), may hold values from -3 to 3
- conv1_weight: bfloat16 [3, 512, 512], P(None, None, 'ch'), may hold values from -0.15625 to 0.15625
- fc2_weight: bfloat16 [2, 128, 512], P(None, None, 'ch'), may hold values from -0.375 to 0.375
- fc2_bias: bfloat16 [2, 512], P(None, 'ch'), may hold values from -3 to 3
- conv2_weight: bfloat16 [3, 512, 512], P(None, None, 'ch'), may hold values from -0.15625 to 0.15625
- conv2_bias: bfloat16 [512], P('ch'), may hold values from -3 to 3
- cotangent: bfloat16 [128, 1024, 512], P('rows', None, 'ch'), may hold values from -6 to 6
Outputs:
- output: bfloat16 [128, 1024, 512], P('rows', None, 'ch')
- grad_frames: bfloat16 [128, 1024, 512], P('rows', None, 'ch')
- grad_style: float32 [128, 4, 128], P('rows')
- grad_fc1_weight: float32 [2, 128, 512], P(None, None, 'ch')
- grad_fc1_bias: float32 [2, 512], P(None, 'ch')
- grad_conv1_weight: float32 [3, 512, 512], P(None, None, 'ch')
- grad_fc2_weight: float32 [2, 128, 512], P(None, None, 'ch')
- grad_fc2_bias: float32 [2, 512], P(None, 'ch')
- grad_conv2_weight: float32 [3, 512, 512], P(None, None, 'ch')
- grad_conv2_bias: float32 [512], P('ch')
The draws below stay inside these ranges and needn't reach their ends.
Inputs may be any that keep to these rules, and one draw needn't show every extreme that they name: `segment_ids`: in each row the ids never fall, begin at 0 and end at 3, and change only at frames that are multiples of 16. `padding`: in each row the zeros, if any, are the last frames.
All inputs are finite; a program needn't handle non-finite values.
Results may differ from the reference program's by a relative error of at most 0.0095.
Values may be sent and summed in bfloat16 or wider, within the bound.
No kernel may reach another device: no remote copies, remote signals or barrier semaphores. Data moves between devices by JAX's collectives and lax.ppermute only.
A program may use at most 320 MiB of HBM per device.

```python
import math
import jax
import jax.numpy as jnp
from jax import lax

CHANNELS = 512
STYLE = 128
FRAMES = 1024
SEGS = 4
ROWS = 128


def draw_segment_ids(key, part):
    key = jax.random.fold_in(key, 11)
    slot_count = FRAMES // 16 - 1
    row_keys = jax.random.split(key, ROWS)
    positions = jnp.arange(FRAMES, dtype=jnp.int32)

    def one_row(row_key):
        ranking = jax.random.permutation(row_key, slot_count)
        chosen = (ranking < SEGS - 1).astype(jnp.int32)
        boundary = jnp.concatenate([jnp.zeros((1,), jnp.int32), chosen])
        starts = boundary[positions // 16] * (positions % 16 == 0).astype(jnp.int32)
        return jnp.cumsum(starts).astype(jnp.int32)
    return jax.vmap(one_row)(row_keys)


def draw_padding(key, part):
    key = jax.random.fold_in(key, 23)
    tails = jax.random.randint(key, (ROWS, 1), 0, FRAMES // 4 + 1)
    positions = jnp.arange(FRAMES, dtype=jnp.int32)[None, :]
    return (positions < FRAMES - tails).astype(jnp.int32)


def shard_levels(rng, shape, shards, low, largest):
    gain = 1.0
    for dim, shards_of in shards:
        heights = jax.random.uniform(jax.random.fold_in(jax.random.fold_in(rng, 6), dim), (shards_of,), jnp.float32, low / len(shards), largest / len(shards))
        gain = gain * jnp.repeat(jnp.exp(heights), shape[dim] // shards_of).reshape((-1,) + (1,) * (len(shape) - 1 - dim))
    return gain


def noise(key, shape, scale, reach, pieces=(), kind=jnp.bfloat16):
    values = jax.random.normal(key, shape, jnp.float32) * scale
    if len(pieces) > 0:
        values = shard_levels(key, shape, pieces, -0.22, 0.18) * values
    return jnp.clip(values, min=-reach, max=reach).astype(kind)


def setup_inputs(seed: int = 0) -> dict:
    streams_of = jax.random.split(jax.random.key(seed), 13)
    return {
        "frames": noise(streams_of[0], (ROWS, FRAMES, CHANNELS), 1.0, 6.0, ((0, 8), (2, 4))),
        "style_vector": noise(streams_of[1], (ROWS, SEGS, STYLE), 1.0, 5.0, ((0, 8),)),
        "segment_ids": draw_segment_ids(jax.random.fold_in(streams_of[12], 71), 0),
        "padding": draw_padding(jax.random.fold_in(streams_of[12], 71), 0),
        "fc1_weight": noise(streams_of[4], (2, STYLE, CHANNELS), (2 * STYLE) ** -0.5, 0.375, ((2, 4),)),
        "fc1_bias": noise(streams_of[5], (2, CHANNELS), 0.5, 3.0, ((1, 4),)),
        "conv1_weight": noise(streams_of[6], (3, CHANNELS, CHANNELS), (3 * CHANNELS) ** -0.5, 0.15625, ((2, 4),)),
        "fc2_weight": noise(streams_of[7], (2, STYLE, CHANNELS), (2 * STYLE) ** -0.5, 0.375, ((2, 4),)),
        "fc2_bias": noise(streams_of[8], (2, CHANNELS), 0.5, 3.0, ((1, 4),)),
        "conv2_weight": noise(streams_of[9], (3, CHANNELS, CHANNELS), (3 * CHANNELS) ** -0.5, 0.15625, ((2, 4),)),
        "conv2_bias": noise(streams_of[10], (CHANNELS,), 0.5, 3.0, ((0, 4),)),
        "cotangent": noise(streams_of[11], (ROWS, FRAMES, CHANNELS), 1.0, 6.0, ((0, 8), (2, 4))),
    }


var_floor = 0.1
inv_root = math.sqrt(0.5)
highest = lax.Precision.HIGHEST

@jax.custom_vjp
def low(v):
    return lax.optimization_barrier(v.astype(jnp.bfloat16)).astype(jnp.float32)

@jax.custom_vjp
def low_back(v):
    return v

def low_keep(v):
    return (low(v), None)

def low_pass(kept, grad):
    return (grad,)

def back_keep(v):
    return (v, None)

def back_low(kept, grad):
    return (low(grad),)
low.defvjp(low_keep, low_pass)
low_back.defvjp(back_keep, back_low)

def shift_down(values):
    return jnp.concatenate([jnp.zeros_like(values[:, :1]), values[:, :-1]], axis=1)

def shift_up(values):
    return jnp.concatenate([values[:, 1:], jnp.zeros_like(values[:, :1])], axis=1)

def joints(segment_ids):
    same_seg = segment_ids[:, 1:] == segment_ids[:, :-1]
    false_col = jnp.zeros_like(same_seg[:, :1])
    left_join = jnp.concatenate([false_col, same_seg], axis=1)[..., None]
    right_join = jnp.concatenate([same_seg, false_col], axis=1)[..., None]
    return (left_join, right_join)

def layout(segment_ids, padding, segments):
    member = (segment_ids[..., None] == jnp.arange(segments, dtype=jnp.int32)).astype(jnp.float32)
    padded_mask = padding.astype(jnp.float32)[..., None]
    return (member, padded_mask)

def adain_act(inputs, style_in, weight_in, bias_in, member, padded_mask):
    weights_seg = member * padded_mask
    counts = jnp.maximum(lax.optimization_barrier(jnp.sum(weights_seg, axis=1)), 1.0)[..., None]
    means = jnp.einsum('rts,rtc->rsc', weights_seg, inputs, precision=highest) / counts
    centered = inputs - jnp.einsum('rts,rsc->rtc', member, means, precision=highest)
    variance = jnp.einsum('rts,rtc->rsc', weights_seg, centered * centered, precision=highest) / counts
    scales = lax.rsqrt(jnp.maximum(variance, var_floor))
    normed = centered * jnp.einsum('rts,rsc->rtc', member, scales, precision=highest)
    project = jnp.einsum('rsi,kic->krsc', style_in, weight_in, precision=highest) + bias_in[:, None, None, :]
    affine = jnp.einsum('rts,krsc->krtc', member, project, precision=highest)
    hidden = (1.0 + affine[0]) * normed + affine[1]
    return jax.nn.silu(hidden) * padded_mask

def convolve_full(inputs, weight, left_join, right_join):
    taps = jnp.einsum('rti,kio->krto', inputs, weight, precision=highest)
    return taps[1] + jnp.where(left_join, shift_down(taps[0]), 0.0) + jnp.where(right_join, shift_up(taps[2]), 0.0)

def block_forward(frames_in, style_in, weights, member, padded_mask, left_join, right_join):
    fc1_w, fc1_b, conv1_w, fc2_w, fc2_b, conv2_w, conv2_b = weights
    first_act = low(adain_act(frames_in, style_in, fc1_w, fc1_b, member, padded_mask))
    first_conv = low_back(convolve_full(first_act, conv1_w, left_join, right_join))
    second_act = low(adain_act(first_conv, style_in, fc2_w, fc2_b, member, padded_mask))
    second_conv = low_back(convolve_full(second_act, conv2_w, left_join, right_join) + conv2_b)
    return (frames_in + second_conv * padded_mask) * inv_root

def reference(frames, style_vector, segment_ids, padding, fc1_weight, fc1_bias, conv1_weight, fc2_weight, fc2_bias, conv2_weight, conv2_bias, cotangent):
    params = tuple((param.astype(jnp.float32) for param in (fc1_weight, fc1_bias, conv1_weight, fc2_weight, fc2_bias, conv2_weight, conv2_bias)))

    def regroup(values):
        return values.reshape((values.shape[0] // 4, 4) + values.shape[1:])

    def block_step(totals, inputs):
        frames_block, style_block, ids_block, pad_block, cot_block = inputs
        member, padded_mask = layout(ids_block, pad_block, SEGS)
        left_join, right_join = joints(ids_block)

        def forward(frames_in, style_in, *weights):
            return block_forward(frames_in, style_in, weights, member, padded_mask, left_join, right_join)
        result, pullback = jax.vjp(forward, frames_block.astype(jnp.float32), style_block.astype(jnp.float32), *params)
        grads = pullback(cot_block.astype(jnp.float32))
        totals = tuple((total + grad for total, grad in zip(totals, grads[2:])))
        return (totals, (result.astype(jnp.bfloat16), grads[0].astype(jnp.bfloat16), grads[1]))
    initial = tuple((jnp.zeros_like(param) for param in params))
    totals, (outputs, grad_frames, grad_style) = lax.scan(block_step, initial, (regroup(frames), regroup(style_vector), regroup(segment_ids), regroup(padding), regroup(cotangent)))
    return (outputs.reshape(frames.shape), grad_frames.reshape(frames.shape), grad_style.reshape(style_vector.shape), totals[0], totals[1], totals[2], totals[3], totals[4], totals[5], totals[6])
```

```python
import functools
import itertools
import math

import jax
import jax.numpy as jnp
from jax import lax
from jax.experimental import pallas as pl
from jax.experimental.pallas import tpu as pltpu
from jax.sharding import PartitionSpec as P

var_floor = 0.1
inv_root = math.sqrt(0.5)
highest = lax.Precision.HIGHEST
BLOCK = 16
NT = (((1,), (1,)), ((), ()))
TN = (((0,), (0,)), ((), ()))


def row_kernel(
    n, segs, style_n, per, start, at_f, at_c, n_prev, z_ref, len_ref, seg_ref, *refs
):
    f_own, c_own = refs[:2]
    recv_f, recv_c = refs[2 : n + 1], refs[n + 1 : 2 * n]
    style_ref, inv_ref, w_hbm = refs[2 * n : 2 * n + 3]
    prev = refs[2 * n + 3 : 2 * n + 3 + n_prev]
    refs = refs[2 * n + 3 + n_prev :]
    o_own, g_own, sum_hbm = refs[:3]
    outs = refs[3 : n + 2]
    dstyle_ref = refs[n + 2]
    fr, ct, res, sh, a3x, a3y, g3, conv, da, acc, coef, w_ref, wt_ref, sum_ref, sems = refs[n + 3 :]

    z = z_ref[0]
    length = len_ref[0]
    frames, chans = fr.shape
    width = chans // n
    blocks = frames // BLOCK
    wide = 3 * chans
    fc_at = 2 * wide
    bias_at = fc_at + 4 * style_n
    row_iota = (
        lax.broadcasted_iota(jnp.int32, (2, 8, chans), 0) * 8
        + lax.broadcasted_iota(jnp.int32, (2, 8, chans), 1)
    )
    edge = lax.broadcasted_iota(jnp.int32, (8, 128), 0)

    def lanes(k):
        return pl.ds(pl.multiple_of(lax.rem(z + n - k, n) * width, width), width)

    def span(b):
        return pl.ds(pl.multiple_of(b * BLOCK, BLOCK), BLOCK)

    def segment(b):
        return seg_ref[0, b + 1]

    def load(ref, b):
        return ref[span(b), :].astype(jnp.float32).reshape(2, 8, chans)

    def flat(v):
        return v.reshape(BLOCK, chans)

    def keep(b, v):
        return jnp.where(row_iota < length - b * BLOCK, v, 0.0)

    def loop(body, unroll=4):
        def step(i, carry):
            for j in range(unroll):
                body(i * unroll + j)
            return carry

        lax.fori_loop(0, blocks // unroll, step, 0)

    def total(slot):
        return jnp.sum(acc[slot], axis=1)

    def put(slot, v):
        coef[slot] = jnp.broadcast_to(v[:, None, :], (segs, 8, chans))

    def fc_rows(layer, k):
        at = fc_at + (2 * layer + k) * style_n
        return slice(at, at + style_n)

    count = itertools.count()

    def copy(src, dst):
        return pltpu.make_async_copy(src, dst, sems.at[next(count)])

    def begin(*copies):
        for c in copies:
            c.start()

    def finish_copies(*copies):
        for c in copies:
            c.wait()

    def pieces(own, start, received, dst):
        yield copy(own.at[z * per + start], dst.at[:, lanes(0)])
        for k, (ref, at) in enumerate(received, 1):
            yield copy(ref.at[pl.ds(at, frames), :], dst.at[:, lanes(k)])

    def weight_copies(layer):
        rows = pl.ds(layer * wide, wide)
        yield copy(w_hbm.at[rows, :], w_ref.at[rows, :])
        for k in range(3):
            rows = pl.ds(layer * wide + k * chans, chans)
            yield copy(w_hbm.at[rows, :], wt_ref.at[layer, :, k * chans : (k + 1) * chans])

    tail_rows = pl.ds(fc_at, w_ref.shape[0] - fc_at)
    layer_rows = [pl.ds(layer * wide, wide) for layer in range(2)]
    get_fr = list(pieces(f_own, start, zip(recv_f, at_f), fr))
    get_ct = list(pieces(c_own, start, zip(recv_c, at_c), ct))
    get_tail = copy(w_hbm.at[tail_rows, :], w_ref.at[tail_rows, :])
    get_w = [list(weight_copies(layer)) for layer in range(2)]
    begin(*get_fr, get_tail, *get_w[0], *get_w[1], *get_ct)
    get_sums = []
    if n_prev:
        get_sums = [copy(prev[2].at[r, :], sum_ref.at[r, :]) for r in (*layer_rows, tail_rows)]
        begin(*get_sums[::-1])
    else:
        sum_ref[...] = jnp.zeros_like(sum_ref)
    put_sums = [copy(sum_ref.at[r, :], sum_hbm.at[r, :]) for r in (*layer_rows, tail_rows)]

    def put_result(which):
        yield copy(res.at[:, lanes(0)], (o_own, g_own)[which].at[z * per + start])
        for k in range(1, n):
            yield copy(res.at[:, lanes(k)], outs[k - 1].at[which, 0])

    for j in range(chans // 128):
        sh[j, 0:8, :] = jnp.zeros((8, 128), jnp.float32)
        sh[j, 8 + frames :, :] = jnp.zeros((8, 128), jnp.float32)

    inv_count = inv_ref[0]
    style = style_ref[0].astype(jnp.float32)
    finish_copies(*get_fr, get_tail)
    biases = w_ref[bias_at : bias_at + BLOCK, :].astype(jnp.float32)

    def project(layer, k):
        proj = jnp.dot(
            style, w_ref[fc_rows(layer, k), :].astype(jnp.float32),
            precision=highest, preferred_element_type=jnp.float32,
        )
        return proj + biases[2 * layer + k : 2 * layer + k + 1]

    def hold(b, v):
        at = pl.ds(pl.multiple_of(b * BLOCK + 8, 8), BLOCK)
        v = flat(v)
        for j in range(chans // 128):
            sh[j, at, :] = v[:, j * 128 : (j + 1) * 128]

    def statistics(src, layer):
        base = layer * 6
        acc[0] = jnp.zeros_like(acc[0])

        def add_values(b):
            v = keep(b, load(src, b))
            acc[0, segment(b)] += v[0] + v[1]

        loop(add_values)
        put(base, total(0) * inv_count)
        acc[0] = jnp.zeros_like(acc[0])

        def add_squares(b):
            s = segment(b)
            c = keep(b, load(src, b) - coef[base, s])
            c = c * c
            acc[0, s] += c[0] + c[1]

        loop(add_squares)
        var = total(0) * inv_count
        rstd = lax.rsqrt(jnp.maximum(var, var_floor))
        put(base + 1, (1.0 + project(layer, 0)) * rstd)
        put(base + 2, project(layer, 1))
        put(base + 3, rstd)
        put(base + 4, jnp.where(var > var_floor, rstd, 0.0) * inv_count)

    def activation(src, layer):
        base = layer * 6

        def body(b):
            s = segment(b)
            u = coef[base + 1, s] * (load(src, b) - coef[base, s]) + coef[base + 2, s]
            hold(b, keep(b, u * (0.5 * jnp.tanh(0.5 * u) + 0.5)))

        loop(body)

    def spread(dst, first):
        last = 2 - first

        def body(b):
            s = segment(b)
            from_row = jnp.where(seg_ref[0, b] == s, 0, 1)
            to_row = jnp.where(seg_ref[0, b + 2] == s, 8, 7)
            for j in range(chans // 128):

                def part(off):
                    return sh[j, pl.ds(b * BLOCK + off, 8), :]

                def store(tap, low, high):
                    at = tap * chans + j * 128
                    v = jnp.concatenate([low, high], axis=0)
                    dst[span(b), at : at + 128] = v.astype(dst.dtype)

                store(first, jnp.where(edge >= from_row, part(7), 0.0), part(15))
                store(1, part(8), part(16))
                store(last, part(9), jnp.where(edge < to_row, part(17), 0.0))

        loop(body)

    tile = min(frames, 1024)

    def convolve(dst, src, layer):
        def body(i, carry):
            at = pl.ds(pl.multiple_of(i * tile, tile), tile)
            dst[at, :] = jnp.dot(
                src[at, :], w_ref[layer * wide : (layer + 1) * wide, :],
                preferred_element_type=jnp.float32,
            )
            return carry

        lax.fori_loop(0, frames // tile, body, 0)

    def input_grad(dst, src, layer):
        def body(i, carry):
            at = pl.ds(pl.multiple_of(i * tile, tile), tile)
            dst[at, :] = lax.dot_general(
                src[at, :], wt_ref[layer], NT, preferred_element_type=jnp.float32
            )
            return carry

        lax.fori_loop(0, frames // tile, body, 0)

    def weight_grad(layer, kept, grads):
        def body(i, carry):
            at = pl.ds(pl.multiple_of(i * 256, 256), 256)
            to = pl.ds(pl.multiple_of(layer * wide + i * 256, 256), 256)
            sum_ref[to, :] += lax.dot_general(
                kept[:, at], grads[:, chans : 2 * chans], TN, preferred_element_type=jnp.float32
            )
            return carry

        lax.fori_loop(0, wide // 256, body, 0)

    def backward(src, layer):
        base = layer * 6
        acc[...] = jnp.zeros_like(acc)

        def body(b):
            s = segment(b)
            c = load(src, b) - coef[base, s]
            u = coef[base + 1, s] * c + coef[base + 2, s]
            sig = 0.5 * jnp.tanh(0.5 * u) + 0.5
            du = keep(b, load(da, b) * (sig * (1.0 + u * (1.0 - sig))))
            da[span(b), :] = flat(du)
            acc[0, s] += du[0] + du[1]
            duc = du * c
            acc[1, s] += duc[0] + duc[1]

        loop(body)
        dbeta = total(0)
        dgain = total(1) * coef[base + 3, :, 0, :]
        put(base + 4, coef[base + 4, :, 0, :] * dgain)
        put(base + 5, inv_count * dbeta)
        for k, d in enumerate((dgain, dbeta)):
            at = fc_rows(layer, k)
            sum_ref[at, :] += lax.dot_general(
                style, d, TN, precision=highest, preferred_element_type=jnp.float32
            )
            dstyle_ref[0] += lax.dot_general(
                d, w_ref[at, :].astype(jnp.float32), NT,
                precision=highest, preferred_element_type=jnp.float32,
            )
        return [jnp.sum(dgain, axis=0, keepdims=True), jnp.sum(dbeta, axis=0, keepdims=True)]

    def value_grad(src, layer, b):
        base = layer * 6
        s = segment(b)
        c = load(src, b) - coef[base, s]
        dv = coef[base + 1, s] * (load(da, b) - (c * coef[base + 4, s] + coef[base + 5, s]))
        return keep(b, dv)

    statistics(fr, 0)
    activation(fr, 0)
    spread(a3x, 0)
    finish_copies(*get_w[0])
    convolve(conv, a3x, 0)
    statistics(conv, 1)
    activation(conv, 1)
    spread(a3y, 0)
    finish_copies(*get_w[1], *get_ct)
    convolve(da, a3y, 1)
    bias = biases[4:5]
    acc[0, 0] = jnp.zeros_like(acc[0, 0])

    def finish(b):
        y = keep(b, load(da, b) + bias[None])
        res[span(b), :] = flat((load(fr, b) + y) * inv_root).astype(res.dtype)
        g = keep(b, load(ct, b) * inv_root).astype(jnp.bfloat16).astype(jnp.float32)
        hold(b, g)
        acc[0, 0] += g[0] + g[1]

    loop(finish)
    bias_sum = jnp.sum(acc[0, 0], axis=0, keepdims=True)
    put_output = list(put_result(0))
    begin(*put_output)

    dstyle_ref[...] = jnp.zeros_like(dstyle_ref)
    spread(g3, 2)
    finish_copies(*get_sums)
    weight_grad(1, a3y, g3)
    begin(put_sums[1])
    input_grad(da, g3, 1)
    rows_two = backward(conv, 1)

    def round_grad(b):
        hold(b, value_grad(conv, 1, b).astype(jnp.bfloat16).astype(jnp.float32))

    loop(round_grad)
    spread(g3, 2)
    weight_grad(0, a3x, g3)
    begin(put_sums[0])
    input_grad(da, g3, 0)
    rows_one = backward(fr, 0)

    sum_ref[bias_at : bias_at + 8, :] += jnp.concatenate(
        rows_one + rows_two + [bias_sum, jnp.zeros((3, chans), jnp.float32)], axis=0
    )
    begin(put_sums[2])
    finish_copies(*put_output)

    def frames_grad(b):
        dv = value_grad(fr, 0, b)
        res[span(b), :] = flat(load(ct, b) * inv_root + dv).astype(res.dtype)

    loop(frames_grad)
    put_grads = list(put_result(1))
    begin(*put_grads)
    finish_copies(*put_grads, *put_sums)


def block_rows(
    n, per, start, z, lengths, seg_blocks, frames, cotangent, recv_f, recv_c, style, inv, weights, prev
):
    frames_n, width = frames.shape[1:]
    chans = width * n
    segs, style_n = style.shape[1:]
    flat_n = weights.shape[0]
    f32 = jnp.float32

    def here(r, *_):
        return (start + r, 0, 0)

    any_space = pl.BlockSpec(memory_space=pl.ANY)
    sums = jax.ShapeDtypeStruct((flat_n, chans), f32)
    piece = jax.ShapeDtypeStruct((2, 1, frames_n, width), jnp.bfloat16)
    in_specs = (
        [any_space] * 2 * n
        + [pl.BlockSpec((1, segs, style_n), here), pl.BlockSpec((1, segs, chans), here)]
        + [any_space] * (1 + len(prev))
    )
    out_specs = [any_space] * (n + 2) + [pl.BlockSpec((1, segs, style_n), lambda *_: (0, 0, 0))]
    out_shape = (
        [jax.ShapeDtypeStruct(frames.shape, jnp.bfloat16)] * 2
        + [sums]
        + [piece] * (n - 1)
        + [jax.ShapeDtypeStruct((1, segs, style_n), f32)]
    )
    scratch = [
        pltpu.VMEM((frames_n, chans), jnp.bfloat16),
        pltpu.VMEM((frames_n, chans), jnp.bfloat16),
        pltpu.VMEM((frames_n, chans), jnp.bfloat16),
        pltpu.VMEM((chans // 128, frames_n + 16, 128), f32),
        pltpu.VMEM((frames_n, 3 * chans), jnp.bfloat16),
        pltpu.VMEM((frames_n, 3 * chans), jnp.bfloat16),
        pltpu.VMEM((frames_n, 3 * chans), jnp.bfloat16),
        pltpu.VMEM((frames_n, chans), f32),
        pltpu.VMEM((frames_n, chans), f32),
        pltpu.VMEM((2, segs, 8, chans), f32),
        pltpu.VMEM((12, segs, 8, chans), f32),
        pltpu.VMEM((flat_n, chans), jnp.bfloat16),
        pltpu.VMEM((2, chans, 3 * chans), jnp.bfloat16),
        pltpu.VMEM((flat_n, chans), f32),
        pltpu.SemaphoreType.DMA((4 * n + 16,)),
    ]
    first_prev = 3 + 2 * n + 3
    return pl.pallas_call(
        functools.partial(
            row_kernel, n, segs, style_n, per, start,
            [at for _, at in recv_f], [at for _, at in recv_c], len(prev),
        ),
        grid_spec=pltpu.PrefetchScalarGridSpec(
            num_scalar_prefetch=3,
            grid=(1,),
            in_specs=in_specs,
            out_specs=out_specs,
            scratch_shapes=scratch,
        ),
        out_shape=out_shape,
        input_output_aliases={first_prev + i: i for i in range(len(prev))},
        compiler_params=pltpu.CompilerParams(vmem_limit_bytes=48 << 20),
        cost_estimate=pl.CostEstimate(
            flops=6 * 2 * 3 * frames_n * chans * chans,
            bytes_accessed=8 * frames_n * chans + 10 * flat_n * chans,
            transcendentals=4 * frames_n * chans,
        ),
    )(
        z, lengths, seg_blocks, frames, cotangent,
        *[v for v, _ in recv_f], *[v for v, _ in recv_c], style, inv, weights, *prev,
    )


def per_device(
    n,
    n_rows,
    frames,
    style_vector,
    segment_ids,
    padding,
    fc1_weight,
    fc1_bias,
    conv1_weight,
    fc2_weight,
    fc2_bias,
    conv2_weight,
    conv2_bias,
    cotangent,
):
    f32 = jnp.float32
    held, frames_n, width = frames.shape
    segs, style_n = style_vector.shape[1:]
    chans = n * width
    per = held // n
    z = lax.axis_index("ch")

    def shift(k):
        return [(i, (i + k) % n) for i in range(n)]

    def send(v, k):
        return lax.ppermute(v, "ch", shift(k))

    def over_ch(v, pieces, axis):
        whole = jnp.concatenate([v] * n, axis=axis)
        size = v.shape[axis]
        for k, piece in enumerate(pieces, 1):
            at = lax.rem(z + n - k, n) * size
            whole = lax.dynamic_update_slice_in_dim(whole, piece, at, axis)
        return whole

    def after(v, others):
        return lax.optimization_barrier((v, others))[0]

    sizes = [3 * chans, 3 * chans, 2 * style_n, 2 * style_n, 2, 2, 1]
    used = sum(sizes)
    padded = -(-used // (16 * n_rows)) * 16 * n_rows
    shard = jnp.concatenate(
        [
            conv1_weight.reshape(-1, width),
            conv2_weight.reshape(-1, width),
            fc1_weight.reshape(-1, width),
            fc2_weight.reshape(-1, width),
            fc1_bias,
            fc2_bias,
            conv2_bias[None],
            jnp.zeros((padded - used, width), conv1_weight.dtype),
        ]
    )
    part = padded // n_rows
    mine = lax.dynamic_slice_in_dim(shard, lax.axis_index("rows") * part, part, 0)

    def piece(v, k, r):
        at = lax.rem(z + k, n) * per + r
        return lax.dynamic_slice_in_dim(v, at, 1, 0)[0]

    recv_f, recv_c, weight_pieces = [], [], []
    for r in range(per):
        got_f, got_c = [], []
        for k in range(1, n):
            f, c = piece(frames, k, r), piece(cotangent, k, r)
            if r == 0:
                both = send(jnp.concatenate([f, mine]), k)
                got_f.append((both, 0))
                weight_pieces.append(both[frames_n:])
                got_c.append((send(c, k), 0))
            else:
                both = send(jnp.concatenate([f, c]), k)
                got_f.append((both, 0))
                got_c.append((both, frames_n))
        recv_f.append(got_f)
        recv_c.append(got_c)
    mine = after(over_ch(mine, weight_pieces, 1), [recv_c[0][0][0]])
    weights = lax.all_gather(mine, "rows", axis=0, tiled=True)

    first = z * per
    my_ids = lax.dynamic_slice_in_dim(segment_ids, first, per, 0)
    my_pad = lax.dynamic_slice_in_dim(padding, first, per, 0)
    my_style = lax.dynamic_slice_in_dim(style_vector, first, per, 0)
    lengths = jnp.sum(my_pad, axis=1).astype(jnp.int32)
    side = jnp.full((per, 1), -1, jnp.int32)
    seg_blocks = jnp.concatenate([side, my_ids[:, ::BLOCK], side], axis=1)
    counts = jnp.sum(
        jnp.where(my_ids[:, :, None] == jnp.arange(segs, dtype=jnp.int32), my_pad[:, :, None], 0),
        axis=1,
    ).astype(f32)
    inv_count = jnp.broadcast_to(
        (1.0 / jnp.maximum(counts, 1.0))[:, :, None], (per, segs, chans)
    )

    prev, back, dstyles = [], [], []
    for r in range(per):
        results = block_rows(
            n, per, r, z[None], lengths[r : r + 1], seg_blocks[r : r + 1], frames, cotangent,
            recv_f[r], recv_c[r], my_style, inv_count, weights, prev,
        )
        prev = list(results[:3])
        dstyles.append(results[n + 2])
        back.append([send(v, n - k) for k, v in enumerate(results[3 : n + 2], 1)])

    output, grad_frames, sums = prev
    for r in range(per):
        for k in range(1, n):
            at = lax.rem(z + k, n) * per + r
            output = lax.dynamic_update_slice_in_dim(output, back[r][k - 1][0], at, 0)
            grad_frames = lax.dynamic_update_slice_in_dim(grad_frames, back[r][k - 1][1], at, 0)

    style_grad = jnp.concatenate(dstyles, axis=0)
    grad_style = over_ch(style_grad, [send(style_grad, k) for k in range(1, n)], 0)

    sums = after(sums, back[0])
    sums = lax.psum_scatter(sums, "rows", scatter_dimension=0, tiled=True)
    sums = after(sums, back[1])
    total = lax.dynamic_slice_in_dim(sums, z * width, width, 1)
    for k in range(1, n):
        at = lax.rem(z + k, n) * width
        total = total + send(lax.dynamic_slice_in_dim(sums, at, width, 1), k)
    total = after(total, back[2])
    grads = lax.all_gather(total, "rows", axis=0, tiled=True)
    splits = [sum(sizes[: i + 1]) for i in range(len(sizes))]
    g1, g2, gf1, gf2, gb1, gb2, gb = [
        grads[end - size : end] for size, end in zip(sizes, splits)
    ]
    return (
        output,
        grad_frames,
        grad_style,
        gf1.reshape(fc1_weight.shape),
        gb1,
        g1.reshape(conv1_weight.shape),
        gf2.reshape(fc2_weight.shape),
        gb2,
        g2.reshape(conv2_weight.shape),
        gb[0],
    )


def solution(mesh):
    return jax.shard_map(
        functools.partial(per_device, mesh.shape["ch"], mesh.shape["rows"]),
        mesh=mesh,
        in_specs=(
            P("rows", None, "ch"),
            P("rows", None, None),
            P("rows", None),
            P("rows", None),
            P(None, None, "ch"),
            P(None, "ch"),
            P(None, None, "ch"),
            P(None, None, "ch"),
            P(None, "ch"),
            P(None, None, "ch"),
            P("ch"),
            P("rows", None, "ch"),
        ),
        out_specs=(
            P("rows", None, "ch"),
            P("rows", None, "ch"),
            P("rows", None, None),
            P(None, None, "ch"),
            P(None, "ch"),
            P(None, None, "ch"),
            P(None, None, "ch"),
            P(None, "ch"),
            P(None, None, "ch"),
            P("ch"),
        ),
        check_vma=False,
    )
```

```python
import functools
import itertools
import math

import jax
import jax.numpy as jnp
from jax import lax
from jax.experimental import pallas as pl
from jax.experimental.pallas import tpu as pltpu
from jax.sharding import PartitionSpec as P

var_floor = 0.1
inv_root = math.sqrt(0.5)
highest = lax.Precision.HIGHEST
COST = 0.5
BLOCK = 16
NT = (((1,), (1,)), ((), ()))
TN = (((0,), (0,)), ((), ()))


def rows_kernel(
    n, segs, style_n, per, first, from_f, from_c, to, has_prev, final, z_ref, len_ref, seg_ref, *refs
):
    f_own, c_own, style_ref, inv_ref, w_hbm = refs[:5]
    refs = refs[5:]
    n_recv = 1 + max(i for i, _ in from_f + from_c)
    recv, refs = refs[: n_recv * (n - 1)], refs[n_recv * (n - 1) :]
    prev, refs = refs[:has_prev], refs[has_prev:]
    sum_hbm, dstyle_ref, o_own, g_own = refs[:4]
    outs = refs[4:-16]
    fr, ct, res, sh, a3x, a3y, g3, conv, da, acc, coef, w_ref, wt_ref, sum_ref = refs[-16:-2]
    round_ref, sems = refs[-2:]

    row = pl.program_id(0)
    last_row = len(from_f) - 1
    z = z_ref[0]
    length = len_ref[row]
    frames, chans = fr.shape
    width = chans // n
    blocks = frames // BLOCK
    wide = 3 * chans
    fc_at = 2 * wide
    bias_at = fc_at + 4 * style_n
    row_iota = (
        lax.broadcasted_iota(jnp.int32, (2, 8, chans), 0) * 8
        + lax.broadcasted_iota(jnp.int32, (2, 8, chans), 1)
    )
    edge = lax.broadcasted_iota(jnp.int32, (8, 128), 0)

    def lanes(k):
        return pl.ds(pl.multiple_of(lax.rem(z + n - k, n) * width, width), width)

    def span(b):
        return pl.ds(pl.multiple_of(b * BLOCK, BLOCK), BLOCK)

    def segment(b):
        return seg_ref[row, b + 1]

    def load(ref, b):
        return ref[span(b), :].astype(jnp.float32).reshape(2, 8, chans)

    def flat(v):
        return v.reshape(BLOCK, chans)

    def keep(b, v):
        return jnp.where(row_iota < length - b * BLOCK, v, 0.0)

    def loop(body, unroll=4):
        def step(i, carry):
            for j in range(unroll):
                body(i * unroll + j)
            return carry

        lax.fori_loop(0, blocks // unroll, step, 0)

    def total(slot):
        return jnp.sum(acc[slot], axis=1)

    def put(slot, v):
        coef[slot] = jnp.broadcast_to(v[:, None, :], (segs, 8, chans))

    def fc_rows(layer, k):
        at = fc_at + (2 * layer + k) * style_n
        return slice(at, at + style_n)

    count = itertools.count()

    def copy(src, dst):
        return pltpu.make_async_copy(src, dst, sems.at[next(count)])

    def begin(*copies):
        for c in copies:
            c.start()

    def finish_copies(*copies):
        for c in copies:
            c.wait()

    def pieces(own, place, at_row, dst):
        which, at = place
        yield copy(own.at[z * per + first + at_row], dst.at[:, lanes(0)])
        for k in range(1, n):
            ref = recv[which * (n - 1) + k - 1]
            yield copy(ref.at[pl.ds(at, frames), :], dst.at[:, lanes(k)])

    def weight_copies(layer):
        rows = pl.ds(layer * wide, wide)
        yield copy(w_hbm.at[rows, :], w_ref.at[rows, :])
        for k in range(3):
            rows = pl.ds(layer * wide + k * chans, chans)
            yield copy(w_hbm.at[rows, :], wt_ref.at[layer, :, k * chans : (k + 1) * chans])

    tail_rows = pl.ds(fc_at, w_ref.shape[0] - fc_at)
    layer_rows = [pl.ds(layer * wide, wide) for layer in range(2)]
    get_tail = copy(w_hbm.at[tail_rows, :], w_ref.at[tail_rows, :])
    get_w = [list(weight_copies(layer)) for layer in range(2)]
    get_sums = []
    if has_prev:
        get_sums = [copy(prev[0].at[r, :], sum_ref.at[r, :]) for r in (*layer_rows, tail_rows)]
    sum_out = round_ref if final else sum_ref
    put_sums = [copy(sum_out.at[r, :], sum_hbm.at[r, :]) for r in (*layer_rows, tail_rows)]

    def send_sums(part):
        rows = (*layer_rows, tail_rows)[part]
        if final:

            def body(i, carry):
                at = pl.ds(pl.multiple_of(rows.start + i * 128, 16), 128)
                round_ref[at, :] = sum_ref[at, :].astype(round_ref.dtype)
                return carry

            lax.fori_loop(0, rows.size // 128, body, 0)
        begin(put_sums[part])

    mark = next(count)
    get = []
    for i in range(last_row + 1):
        count = itertools.count(mark)
        get_fr = list(pieces(f_own, from_f[i], i, fr))
        get_ct = list(pieces(c_own, from_c[i], i, ct))
        pl.when(row == i)(functools.partial(begin, *get_fr, *get_ct))

    @pl.when(row == 0)
    def _():
        begin(get_tail, *get_w[0], *get_w[1], *get_sums[::-1])
        if not has_prev:
            sum_ref[...] = jnp.zeros_like(sum_ref)

    mark_out = next(count)

    def put_result(which, at_row):
        yield copy(res.at[:, lanes(0)], (o_own, g_own)[which].at[z * per + first + at_row])
        array, at = to[at_row]
        for k in range(1, n):
            dst = outs[array * (n - 1) + k - 1].at[2 * at + which]
            yield copy(res.at[:, lanes(k)], dst)

    def start_result(which):
        nonlocal count
        for i in range(last_row + 1):
            count = itertools.count(mark_out + n * which)
            copies = list(put_result(which, i))
            pl.when(row == i)(functools.partial(begin, *copies))
        return copies

    def on_row(i, *copies, act):
        pl.when(row == i)(functools.partial(act, *copies))

    for j in range(chans // 128):
        sh[j, 0:8, :] = jnp.zeros((8, 128), jnp.float32)
        sh[j, 8 + frames :, :] = jnp.zeros((8, 128), jnp.float32)

    inv_count = inv_ref[0]
    style = style_ref[0].astype(jnp.float32)
    finish_copies(*get_fr)
    on_row(0, get_tail, act=finish_copies)
    biases = w_ref[bias_at : bias_at + BLOCK, :].astype(jnp.float32)

    def project(layer, k):
        proj = jnp.dot(
            style, w_ref[fc_rows(layer, k), :].astype(jnp.float32),
            precision=highest, preferred_element_type=jnp.float32,
        )
        return proj + biases[2 * layer + k : 2 * layer + k + 1]

    def hold(b, v):
        at = pl.ds(pl.multiple_of(b * BLOCK + 8, 8), BLOCK)
        v = flat(v)
        for j in range(chans // 128):
            sh[j, at, :] = v[:, j * 128 : (j + 1) * 128]

    def statistics(src, layer):
        base = layer * 6
        acc[0] = jnp.zeros_like(acc[0])

        def add_values(b):
            v = keep(b, load(src, b))
            acc[0, segment(b)] += v[0] + v[1]

        loop(add_values)
        put(base, total(0) * inv_count)
        acc[0] = jnp.zeros_like(acc[0])

        def add_squares(b):
            s = segment(b)
            c = keep(b, load(src, b) - coef[base, s])
            c = c * c
            acc[0, s] += c[0] + c[1]

        loop(add_squares)
        var = total(0) * inv_count
        rstd = lax.rsqrt(jnp.maximum(var, var_floor))
        put(base + 1, (1.0 + project(layer, 0)) * rstd)
        put(base + 2, project(layer, 1))
        put(base + 3, rstd)
        put(base + 4, jnp.where(var > var_floor, rstd, 0.0) * inv_count)

    def activation(src, layer):
        base = layer * 6

        def body(b):
            s = segment(b)
            u = coef[base + 1, s] * (load(src, b) - coef[base, s]) + coef[base + 2, s]
            hold(b, keep(b, u * (0.5 * jnp.tanh(0.5 * u) + 0.5)))

        loop(body)

    def spread(dst, first):
        last = 2 - first

        def body(b):
            s = segment(b)
            from_row = jnp.where(seg_ref[row, b] == s, 0, 1)
            to_row = jnp.where(seg_ref[row, b + 2] == s, 8, 7)
            for j in range(chans // 128):

                def part(off):
                    return sh[j, pl.ds(b * BLOCK + off, 8), :]

                def store(tap, low, high):
                    at = tap * chans + j * 128
                    v = jnp.concatenate([low, high], axis=0)
                    dst[span(b), at : at + 128] = v.astype(dst.dtype)

                store(first, jnp.where(edge >= from_row, part(7), 0.0), part(15))
                store(1, part(8), part(16))
                store(last, part(9), jnp.where(edge < to_row, part(17), 0.0))

        loop(body)

    tile = min(frames, 1024)

    def convolve(dst, src, layer):
        def body(i, carry):
            at = pl.ds(pl.multiple_of(i * tile, tile), tile)
            dst[at, :] = jnp.dot(
                src[at, :], w_ref[layer * wide : (layer + 1) * wide, :],
                preferred_element_type=jnp.float32,
            )
            return carry

        lax.fori_loop(0, frames // tile, body, 0)

    def input_grad(dst, src, layer):
        def body(i, carry):
            at = pl.ds(pl.multiple_of(i * tile, tile), tile)
            dst[at, :] = lax.dot_general(
                src[at, :], wt_ref[layer], NT, preferred_element_type=jnp.float32
            )
            return carry

        lax.fori_loop(0, frames // tile, body, 0)

    def weight_grad(layer, kept, grads):
        def body(i, carry):
            at = pl.ds(pl.multiple_of(i * 256, 256), 256)
            to = pl.ds(pl.multiple_of(layer * wide + i * 256, 256), 256)
            sum_ref[to, :] += lax.dot_general(
                kept[:, at], grads[:, chans : 2 * chans], TN, preferred_element_type=jnp.float32
            )
            return carry

        lax.fori_loop(0, wide // 256, body, 0)

    def backward(src, layer):
        base = layer * 6
        acc[...] = jnp.zeros_like(acc)

        def body(b):
            s = segment(b)
            c = load(src, b) - coef[base, s]
            u = coef[base + 1, s] * c + coef[base + 2, s]
            sig = 0.5 * jnp.tanh(0.5 * u) + 0.5
            du = keep(b, load(da, b) * (sig * (1.0 + u * (1.0 - sig))))
            da[span(b), :] = flat(du)
            acc[0, s] += du[0] + du[1]
            duc = du * c
            acc[1, s] += duc[0] + duc[1]

        loop(body)
        dbeta = total(0)
        dgain = total(1) * coef[base + 3, :, 0, :]
        put(base + 4, coef[base + 4, :, 0, :] * dgain)
        put(base + 5, inv_count * dbeta)
        for k, d in enumerate((dgain, dbeta)):
            at = fc_rows(layer, k)
            sum_ref[at, :] += lax.dot_general(
                style, d, TN, precision=highest, preferred_element_type=jnp.float32
            )
            dstyle_ref[0] += lax.dot_general(
                d, w_ref[at, :].astype(jnp.float32), NT,
                precision=highest, preferred_element_type=jnp.float32,
            )
        return [jnp.sum(dgain, axis=0, keepdims=True), jnp.sum(dbeta, axis=0, keepdims=True)]

    def value_grad(src, layer, b):
        base = layer * 6
        s = segment(b)
        c = load(src, b) - coef[base, s]
        dv = coef[base + 1, s] * (load(da, b) - (c * coef[base + 4, s] + coef[base + 5, s]))
        return keep(b, dv)

    statistics(fr, 0)
    activation(fr, 0)
    spread(a3x, 0)
    on_row(0, *get_w[0], act=finish_copies)
    convolve(conv, a3x, 0)
    statistics(conv, 1)
    activation(conv, 1)
    spread(a3y, 0)
    on_row(0, *get_w[1], act=finish_copies)
    finish_copies(*get_ct)
    convolve(da, a3y, 1)
    bias = biases[4:5]
    acc[0, 0] = jnp.zeros_like(acc[0, 0])

    def finish(b):
        y = keep(b, load(da, b) + bias[None])
        res[span(b), :] = flat((load(fr, b) + y) * inv_root).astype(res.dtype)
        g = keep(b, load(ct, b) * inv_root).astype(jnp.bfloat16).astype(jnp.float32)
        hold(b, g)
        acc[0, 0] += g[0] + g[1]

    loop(finish)
    bias_sum = jnp.sum(acc[0, 0], axis=0, keepdims=True)
    put_output = start_result(0)

    dstyle_ref[...] = jnp.zeros_like(dstyle_ref)
    spread(g3, 2)
    on_row(0, *get_sums, act=finish_copies)
    weight_grad(1, a3y, g3)
    on_row(last_row, 1, act=send_sums)
    input_grad(da, g3, 1)
    rows_two = backward(conv, 1)

    def round_grad(b):
        hold(b, value_grad(conv, 1, b).astype(jnp.bfloat16).astype(jnp.float32))

    loop(round_grad)
    spread(g3, 2)
    weight_grad(0, a3x, g3)
    on_row(last_row, 0, act=send_sums)
    input_grad(da, g3, 0)
    rows_one = backward(fr, 0)

    sum_ref[bias_at : bias_at + 8, :] += jnp.concatenate(
        rows_one + rows_two + [bias_sum, jnp.zeros((3, chans), jnp.float32)], axis=0
    )
    on_row(last_row, 2, act=send_sums)
    finish_copies(*put_output)

    def frames_grad(b):
        dv = value_grad(fr, 0, b)
        res[span(b), :] = flat(load(ct, b) * inv_root + dv).astype(res.dtype)

    loop(frames_grad)
    finish_copies(*start_result(1))
    on_row(last_row, *put_sums, act=finish_copies)


def block_rows(
    n, per, first, z, lengths, seg_blocks, frames, cotangent, style, inv, weights,
    recv, from_f, from_c, to, prev, final,
):
    frames_n, width = frames.shape[1:]
    chans = width * n
    segs, style_n = style.shape[1:]
    flat_n = weights.shape[0]
    rows = len(to)
    f32 = jnp.float32

    def here(r, *_):
        return (first + r, 0, 0)

    received = [v for group in recv for v in group]
    any_space = pl.BlockSpec(memory_space=pl.ANY)
    in_specs = (
        [any_space] * 2
        + [pl.BlockSpec((1, segs, style_n), here), pl.BlockSpec((1, segs, chans), here)]
        + [any_space] * (1 + len(received) + len(prev))
    )
    out_shape = [
        jax.ShapeDtypeStruct((flat_n, chans), jnp.bfloat16 if final else f32),
        jax.ShapeDtypeStruct((rows, segs, style_n), f32),
    ]
    out_shape += [jax.ShapeDtypeStruct(frames.shape, jnp.bfloat16)] * 2
    for i in range(1 + max(i for i, _ in to)):
        size = 2 * sum(j == i for j, _ in to)
        out_shape += [jax.ShapeDtypeStruct((size, frames_n, width), jnp.bfloat16)] * (n - 1)
    out_specs = [any_space] * len(out_shape)
    out_specs[1] = pl.BlockSpec((1, segs, style_n), lambda r, *_: (r, 0, 0))
    scratch = [
        pltpu.VMEM((frames_n, chans), jnp.bfloat16),
        pltpu.VMEM((frames_n, chans), jnp.bfloat16),
        pltpu.VMEM((frames_n, chans), jnp.bfloat16),
        pltpu.VMEM((chans // 128, frames_n + 16, 128), f32),
        pltpu.VMEM((frames_n, 3 * chans), jnp.bfloat16),
        pltpu.VMEM((frames_n, 3 * chans), jnp.bfloat16),
        pltpu.VMEM((frames_n, 3 * chans), jnp.bfloat16),
        pltpu.VMEM((frames_n, chans), f32),
        pltpu.VMEM((frames_n, chans), f32),
        pltpu.VMEM((2, segs, 8, chans), f32),
        pltpu.VMEM((12, segs, 8, chans), f32),
        pltpu.VMEM((flat_n, chans), jnp.bfloat16),
        pltpu.VMEM((2, chans, 3 * chans), jnp.bfloat16),
        pltpu.VMEM((flat_n, chans), f32),
        pltpu.VMEM((flat_n if final else 16, chans), jnp.bfloat16),
        pltpu.SemaphoreType.DMA((4 * n + 16,)),
    ]
    first_prev = 3 + 5 + len(received)
    return pl.pallas_call(
        functools.partial(
            rows_kernel, n, segs, style_n, per, first, from_f, from_c, to, len(prev), final,
        ),
        grid_spec=pltpu.PrefetchScalarGridSpec(
            num_scalar_prefetch=3,
            grid=(rows,),
            in_specs=in_specs,
            out_specs=out_specs,
            scratch_shapes=scratch,
        ),
        out_shape=out_shape,
        input_output_aliases={first_prev + i: 1 + i for i in range(1, len(prev))},
        compiler_params=pltpu.CompilerParams(vmem_limit_bytes=48 << 20),
        cost_estimate=pl.CostEstimate(
            flops=int(COST * rows * 6 * 2 * 3 * frames_n * chans * chans), bytes_accessed=1000000,
            transcendentals=0,
        ),
    )(
        z, lengths, seg_blocks, frames, cotangent, style, inv, weights,
        *received, *prev,
    )


def pack_kernel(n, per, part, z_ref, i_ref, frames, conv1, conv2, fc1, fc2, biases, *refs):
    outs, mine = refs[: n - 1], refs[n - 1]
    stage, rows, sems = refs[n:]
    count = itertools.count()

    def copy(src, dst):
        c = pltpu.make_async_copy(src, dst, sems.at[next(count)])
        c.start()
        return c

    frames_n = frames.shape[1]
    at, staged = 0, []
    for ref in (conv1, conv2, fc1, fc2, biases):
        staged.append(copy(ref, stage.at[pl.ds(at, ref.shape[0]), :]))
        at += ref.shape[0]
    read = []
    for k in range(1, n):
        read.append(copy(frames.at[lax.rem(z_ref[0] + k, n) * per], rows.at[k - 1]))
    sent = []
    if at < stage.shape[0]:
        stage[at:, :] = jnp.zeros((stage.shape[0] - at, stage.shape[1]), stage.dtype)
    for c in staged:
        c.wait()
    src = stage.at[pl.ds(pl.multiple_of(i_ref[0] * part, 16), part), :]
    sent.append(copy(src, mine))
    for k in range(1, n):
        sent.append(copy(src, outs[k - 1].at[pl.ds(frames_n, part), :]))
        read[k - 1].wait()
        sent.append(copy(rows.at[k - 1], outs[k - 1].at[pl.ds(0, frames_n), :]))
    for c in sent:
        c.wait()


def pack(n, n_rows, per, z, i, frames, weights):
    frames_n, width = frames.shape[1:]
    rows = sum(v.shape[0] for v in weights)
    padded = -(-rows // (16 * n_rows)) * 16 * n_rows
    part = padded // n_rows
    any_space = pl.BlockSpec(memory_space=pl.ANY)
    return pl.pallas_call(
        functools.partial(pack_kernel, n, per, part),
        grid_spec=pltpu.PrefetchScalarGridSpec(
            num_scalar_prefetch=2,
            grid=(1,),
            in_specs=[any_space] * (1 + len(weights)),
            out_specs=[any_space] * n,
            scratch_shapes=[
                pltpu.VMEM((padded, width), jnp.bfloat16),
                pltpu.VMEM((n - 1, frames_n, width), jnp.bfloat16),
                pltpu.SemaphoreType.DMA((3 * n + len(weights),)),
            ],
        ),
        out_shape=[jax.ShapeDtypeStruct((frames_n + part, width), jnp.bfloat16)] * (n - 1)
        + [jax.ShapeDtypeStruct((part, width), jnp.bfloat16)],
        compiler_params=pltpu.CompilerParams(vmem_limit_bytes=56 << 20),
        cost_estimate=pl.CostEstimate(flops=0, bytes_accessed=6 * padded * width, transcendentals=0),
    )(z, i, frames, *weights)


def per_device(
    n,
    n_rows,
    frames,
    style_vector,
    segment_ids,
    padding,
    fc1_weight,
    fc1_bias,
    conv1_weight,
    fc2_weight,
    fc2_bias,
    conv2_weight,
    conv2_bias,
    cotangent,
):
    f32 = jnp.float32
    held, frames_n, width = frames.shape
    segs, style_n = style_vector.shape[1:]
    chans = n * width
    per = held // n
    z = lax.axis_index("ch")

    def shift(k):
        return [(i, (i + k) % n) for i in range(n)]

    def send(v, k, what):
        with jax.named_scope(what):
            return lax.ppermute(v, "ch", shift(k))

    def over_ch(v, pieces, axis):
        whole = jnp.concatenate([v] * n, axis=axis)
        size = v.shape[axis]
        for k, piece in enumerate(pieces, 1):
            at = lax.rem(z + n - k, n) * size
            whole = lax.dynamic_update_slice_in_dim(whole, piece, at, axis)
        return whole

    def after(v, others):
        return lax.optimization_barrier((v, others))[0]

    sizes = [3 * chans, 3 * chans, 2 * style_n, 2 * style_n, 2, 2, 1]
    used = sum(sizes)
    biases = jnp.concatenate(
        [fc1_bias, fc2_bias, conv2_bias[None], jnp.zeros((11, width), fc1_bias.dtype)]
    )
    shard = [v.reshape(-1, width) for v in (conv1_weight, conv2_weight, fc1_weight, fc2_weight)]
    *bundles, mine = pack(
        n, n_rows, per, z[None], lax.axis_index("rows")[None], frames, shard + [biases]
    )

    def piece(v, k, r):
        at = lax.rem(z + k, n) * per + r
        return lax.dynamic_slice_in_dim(v, at, 1, 0)[0]

    def swap(v, what):
        with jax.named_scope(what):
            return lax.all_to_all(v, "ch", 0, 0)

    def of_row(v, r):
        return v.reshape(n, per, frames_n, width)[:, r]

    def bundle(*names):
        return [
            jnp.concatenate([piece({"f": frames, "c": cotangent}[v], k, r) for v, r in names])
            for k in range(1, n)
        ]

    def fetch(what, pieces):
        return [send(v, k, what) for k, v in enumerate(pieces, 1)]

    half = per // 2
    early = [(v, r) for r in range(half) for v in "fc"]
    late = [(v, r) for r in range(half, per) for v in "fc"]
    got_a = fetch("frames_0", bundles)
    got_b = fetch("inputs_1", bundle(*early[1:]))
    got_c = fetch("inputs_2", after(bundle(*late), got_b))
    mine = over_ch(mine, [v[frames_n:] for v in got_a], 1)
    mine = after(mine, [got_b[0], got_b[2]])
    weights = lax.all_gather(mine, "rows", axis=0, tiled=True)

    first = z * per
    my_ids = lax.dynamic_slice_in_dim(segment_ids, first, per, 0)
    my_pad = lax.dynamic_slice_in_dim(padding, first, per, 0)
    my_style = lax.dynamic_slice_in_dim(style_vector, first, per, 0)
    lengths = jnp.sum(my_pad, axis=1).astype(jnp.int32)
    side = jnp.full((per, 1), -1, jnp.int32)
    seg_blocks = jnp.concatenate([side, my_ids[:, ::BLOCK], side], axis=1)
    counts = jnp.sum(
        jnp.where(my_ids[:, :, None] == jnp.arange(segs, dtype=jnp.int32), my_pad[:, :, None], 0),
        axis=1,
    ).astype(f32)
    inv_count = jnp.broadcast_to(
        (1.0 / jnp.maximum(counts, 1.0))[:, :, None], (per, segs, chans)
    )

    def run(first, count, recv, from_f, from_c, to, prev):
        ids, sizes = seg_blocks[first : first + count], lengths[first : first + count]
        return block_rows(
            n, per, first, z[None], sizes, ids, frames, cotangent, my_style, inv_count, weights,
            recv, from_f, from_c, to, prev, bool(prev),
        )

    def spots(group, skip, which, rows):
        return [(group, (2 * r + which - skip) * frames_n) for r in rows]

    sums, dstyle_a, *rest = run(
        0, half, [got_a, got_b], [(0, 0)] + spots(1, 1, 0, range(1, half)),
        spots(1, 1, 1, range(half)), [(0, r) for r in range(half)], [],
    )
    own, pieces = rest[:2], after(rest[2:], got_c)
    back = [[send(v, n - k, "results_0") for k, v in enumerate(pieces, 1)]]
    others = range(per - half)
    sums, dstyle_b, *rest = run(
        half, per - half, [got_c], spots(0, 0, 0, others), spots(0, 0, 1, others),
        [(r, 0) for r in others], [sums, *own],
    )
    own, pieces = rest[:2], rest[2:]
    for r in others:
        group = pieces[r * (n - 1) : (r + 1) * (n - 1)]
        if r == 0:
            group = after(group, back[0][2])
        back.append([send(v, n - k, f"results_{half + r}") for k, v in enumerate(group, 1)])
    dstyles = [dstyle_a, dstyle_b]

    sums = after(sums, back[0][:2])
    sums = lax.psum_scatter(sums, "rows", scatter_dimension=0, tiled=True)
    sums = after(sums, [back[1][0], back[1][2]])
    style_grad = jnp.concatenate(dstyles, axis=0).reshape(per * segs, style_n).astype(sums.dtype)

    def share(k):
        at = lax.rem(z + k, n) * width
        return lax.dynamic_slice_in_dim(sums, at, width, 1)

    got = [send(jnp.concatenate([share(k), style_grad]), k, "sums") for k in range(1, n)]
    part = sums.shape[0]
    total = share(0).astype(f32)
    for v in got:
        total = total + v[:part].astype(f32)
    grad_style = over_ch(style_grad, [v[part:] for v in got], 0)
    grad_style = grad_style.astype(f32).reshape(style_vector.shape)
    total = after(total, [back[1][1], back[2][0]])
    grads = lax.all_gather(total, "rows", axis=0, tiled=True)
    splits = [sum(sizes[: i + 1]) for i in range(len(sizes))]
    g1, g2, gf1, gf2, gb1, gb2, gb = [
        grads[end - size : end] for size, end in zip(sizes, splits)
    ]
    grads = [
        gf1.reshape(fc1_weight.shape),
        gb1,
        g1.reshape(conv1_weight.shape),
        gf2.reshape(fc2_weight.shape),
        gb2,
        g2.reshape(conv2_weight.shape),
        gb[0],
    ]

    results = [v.reshape(n, per, frames_n, width) for v in own]
    for r in range(per):
        if r == per - 1:
            grads, results = lax.optimization_barrier((grads, results))
        group, at = (0, r) if r < half else (r - half + 1, 0)
        for which in range(2):
            for k, v in enumerate(back[group], 1):
                results[which] = lax.dynamic_update_slice(
                    results[which], v[None, None, 2 * at + which], (lax.rem(z + k, n), r, 0, 0)
                )
    output, grad_frames = [v.reshape(frames.shape) for v in results]
    return (output, grad_frames, grad_style, *grads)


def solution(mesh):
    return jax.shard_map(
        functools.partial(per_device, mesh.shape["ch"], mesh.shape["rows"]),
        mesh=mesh,
        in_specs=(
            P("rows", None, "ch"),
            P("rows", None, None),
            P("rows", None),
            P("rows", None),
            P(None, None, "ch"),
            P(None, "ch"),
            P(None, None, "ch"),
            P(None, None, "ch"),
            P(None, "ch"),
            P(None, None, "ch"),
            P("ch"),
            P("rows", None, "ch"),
        ),
        out_specs=(
            P("rows", None, "ch"),
            P("rows", None, "ch"),
            P("rows", None, None),
            P(None, None, "ch"),
            P(None, "ch"),
            P(None, None, "ch"),
            P(None, None, "ch"),
            P(None, "ch"),
            P(None, None, "ch"),
            P("ch"),
        ),
        check_vma=False,
    )
```

```python
import functools
import itertools
import math

import jax
import jax.numpy as jnp
from jax import lax
from jax.experimental import pallas as pl
from jax.experimental.pallas import tpu as pltpu
from jax.sharding import PartitionSpec as P

var_floor = 0.1
inv_root = math.sqrt(0.5)
highest = lax.Precision.HIGHEST
COST = 0.5
BLOCK = 16
NT = (((1,), (1,)), ((), ()))
TN = (((0,), (0,)), ((), ()))


def rows_kernel(
    n, segs, style_n, per, first, from_f, from_c, to, has_prev, final, z_ref, len_ref, seg_ref, *refs
):
    f_own, c_own, style_ref, inv_ref, w_hbm = refs[:5]
    refs = refs[5:]
    n_recv = 1 + max(i for i, _ in from_f + from_c)
    recv, refs = refs[: n_recv * (n - 1)], refs[n_recv * (n - 1) :]
    prev, refs = refs[:has_prev], refs[has_prev:]
    sum_hbm, dstyle_ref, o_own, g_own = refs[:4]
    outs = refs[4:-16]
    fr, ct, res, sh, a3x, a3y, g3, conv, da, acc, coef, w_ref, wt_ref, sum_ref = refs[-16:-2]
    round_ref, sems = refs[-2:]

    row = pl.program_id(0)
    last_row = len(from_f) - 1
    z = z_ref[0]
    length = len_ref[row]
    frames, chans = fr.shape
    width = chans // n
    blocks = frames // BLOCK
    wide = 3 * chans
    fc_at = 2 * wide
    bias_at = fc_at + 4 * style_n
    row_iota = (
        lax.broadcasted_iota(jnp.int32, (2, 8, chans), 0) * 8
        + lax.broadcasted_iota(jnp.int32, (2, 8, chans), 1)
    )
    edge = lax.broadcasted_iota(jnp.int32, (8, 128), 0)

    def lanes(k):
        return pl.ds(pl.multiple_of(lax.rem(z + n - k, n) * width, width), width)

    def span(b):
        return pl.ds(pl.multiple_of(b * BLOCK, BLOCK), BLOCK)

    def segment(b):
        return seg_ref[row, b + 1]

    def load(ref, b):
        return ref[span(b), :].astype(jnp.float32).reshape(2, 8, chans)

    def flat(v):
        return v.reshape(BLOCK, chans)

    def keep(b, v):
        return jnp.where(row_iota < length - b * BLOCK, v, 0.0)

    def loop(body, unroll=4):
        def step(i, carry):
            for j in range(unroll):
                body(i * unroll + j)
            return carry

        lax.fori_loop(0, blocks // unroll, step, 0)

    def total(slot):
        return jnp.sum(acc[slot], axis=1)

    def put(slot, v):
        coef[slot] = jnp.broadcast_to(v[:, None, :], (segs, 8, chans))

    def fc_rows(layer, k):
        at = fc_at + (2 * layer + k) * style_n
        return slice(at, at + style_n)

    count = itertools.count()

    def copy(src, dst):
        return pltpu.make_async_copy(src, dst, sems.at[next(count)])

    def begin(*copies):
        for c in copies:
            c.start()

    def finish_copies(*copies):
        for c in copies:
            c.wait()

    def pieces(own, place, at_row, dst):
        which, at = place
        yield copy(own.at[z * per + first + at_row], dst.at[:, lanes(0)])
        for k in range(1, n):
            ref = recv[which * (n - 1) + k - 1]
            yield copy(ref.at[pl.ds(at, frames), :], dst.at[:, lanes(k)])

    def weight_copies(layer):
        rows = pl.ds(layer * wide, wide)
        yield copy(w_hbm.at[rows, :], w_ref.at[rows, :])
        for k in range(3):
            rows = pl.ds(layer * wide + k * chans, chans)
            yield copy(w_hbm.at[rows, :], wt_ref.at[layer, :, k * chans : (k + 1) * chans])

    tail_rows = pl.ds(fc_at, w_ref.shape[0] - fc_at)
    layer_rows = [pl.ds(layer * wide, wide) for layer in range(2)]
    get_tail = copy(w_hbm.at[tail_rows, :], w_ref.at[tail_rows, :])
    get_w = [list(weight_copies(layer)) for layer in range(2)]
    get_sums = []
    if has_prev:
        get_sums = [copy(prev[0].at[r, :], sum_ref.at[r, :]) for r in (*layer_rows, tail_rows)]
    sum_out = round_ref if final else sum_ref
    put_sums = [copy(sum_out.at[r, :], sum_hbm.at[r, :]) for r in (*layer_rows, tail_rows)]

    def send_sums(part):
        rows = (*layer_rows, tail_rows)[part]
        if final:

            def body(i, carry):
                at = pl.ds(pl.multiple_of(rows.start + i * 128, 16), 128)
                round_ref[at, :] = sum_ref[at, :].astype(round_ref.dtype)
                return carry

            lax.fori_loop(0, rows.size // 128, body, 0)
        begin(put_sums[part])

    mark = next(count)
    get = []
    for i in range(last_row + 1):
        count = itertools.count(mark)
        get_fr = list(pieces(f_own, from_f[i], i, fr))
        get_ct = list(pieces(c_own, from_c[i], i, ct))
        pl.when(row == i)(functools.partial(begin, *get_fr, *get_ct))

    @pl.when(row == 0)
    def _():
        begin(get_tail, *get_w[0], *get_w[1], *get_sums[::-1])
        if not has_prev:
            sum_ref[...] = jnp.zeros_like(sum_ref)

    mark_out = next(count)

    def put_result(which, at_row):
        yield copy(res.at[:, lanes(0)], (o_own, g_own)[which].at[z * per + first + at_row])
        array, at = to[at_row]
        for k in range(1, n):
            dst = outs[array * (n - 1) + k - 1].at[2 * at + which]
            yield copy(res.at[:, lanes(k)], dst)

    def start_result(which):
        nonlocal count
        for i in range(last_row + 1):
            count = itertools.count(mark_out + n * which)
            copies = list(put_result(which, i))
            pl.when(row == i)(functools.partial(begin, *copies))
        return copies

    def on_row(i, *copies, act):
        pl.when(row == i)(functools.partial(act, *copies))

    for j in range(chans // 128):
        sh[j, 0:8, :] = jnp.zeros((8, 128), jnp.float32)
        sh[j, 8 + frames :, :] = jnp.zeros((8, 128), jnp.float32)

    inv_count = inv_ref[0]
    style = style_ref[0].astype(jnp.float32)
    finish_copies(*get_fr)
    on_row(0, get_tail, act=finish_copies)
    biases = w_ref[bias_at : bias_at + BLOCK, :].astype(jnp.float32)

    def project(layer, k):
        proj = jnp.dot(
            style, w_ref[fc_rows(layer, k), :].astype(jnp.float32),
            precision=highest, preferred_element_type=jnp.float32,
        )
        return proj + biases[2 * layer + k : 2 * layer + k + 1]

    def hold(b, v):
        at = pl.ds(pl.multiple_of(b * BLOCK + 8, 8), BLOCK)
        v = flat(v)
        for j in range(chans // 128):
            sh[j, at, :] = v[:, j * 128 : (j + 1) * 128]

    def statistics(src, layer):
        base = layer * 6
        acc[0] = jnp.zeros_like(acc[0])

        def add_values(b):
            v = keep(b, load(src, b))
            acc[0, segment(b)] += v[0] + v[1]

        loop(add_values)
        put(base, total(0) * inv_count)
        acc[0] = jnp.zeros_like(acc[0])

        def add_squares(b):
            s = segment(b)
            c = keep(b, load(src, b) - coef[base, s])
            c = c * c
            acc[0, s] += c[0] + c[1]

        loop(add_squares)
        var = total(0) * inv_count
        rstd = lax.rsqrt(jnp.maximum(var, var_floor))
        put(base + 1, (1.0 + project(layer, 0)) * rstd)
        put(base + 2, project(layer, 1))
        put(base + 3, rstd)
        put(base + 4, jnp.where(var > var_floor, rstd, 0.0) * inv_count)

    def activation(src, layer):
        base = layer * 6

        def body(b):
            s = segment(b)
            u = coef[base + 1, s] * (load(src, b) - coef[base, s]) + coef[base + 2, s]
            hold(b, keep(b, u * (0.5 * jnp.tanh(0.5 * u) + 0.5)))

        loop(body)

    def spread(dst, first):
        last = 2 - first

        def body(b):
            s = segment(b)
            from_row = jnp.where(seg_ref[row, b] == s, 0, 1)
            to_row = jnp.where(seg_ref[row, b + 2] == s, 8, 7)
            for j in range(chans // 128):

                def part(off):
                    return sh[j, pl.ds(b * BLOCK + off, 8), :]

                def store(tap, low, high):
                    at = tap * chans + j * 128
                    v = jnp.concatenate([low, high], axis=0)
                    dst[span(b), at : at + 128] = v.astype(dst.dtype)

                store(first, jnp.where(edge >= from_row, part(7), 0.0), part(15))
                store(1, part(8), part(16))
                store(last, part(9), jnp.where(edge < to_row, part(17), 0.0))

        loop(body)

    tile = min(frames, 1024)

    def convolve(dst, src, layer):
        def body(i, carry):
            at = pl.ds(pl.multiple_of(i * tile, tile), tile)
            dst[at, :] = jnp.dot(
                src[at, :], w_ref[layer * wide : (layer + 1) * wide, :],
                preferred_element_type=jnp.float32,
            )
            return carry

        lax.fori_loop(0, frames // tile, body, 0)

    def input_grad(dst, src, layer):
        def body(i, carry):
            at = pl.ds(pl.multiple_of(i * tile, tile), tile)
            dst[at, :] = lax.dot_general(
                src[at, :], wt_ref[layer], NT, preferred_element_type=jnp.float32
            )
            return carry

        lax.fori_loop(0, frames // tile, body, 0)

    def weight_grad(layer, kept, grads):
        def body(i, carry):
            at = pl.ds(pl.multiple_of(i * 256, 256), 256)
            to = pl.ds(pl.multiple_of(layer * wide + i * 256, 256), 256)
            sum_ref[to, :] += lax.dot_general(
                kept[:, at], grads[:, chans : 2 * chans], TN, preferred_element_type=jnp.float32
            )
            return carry

        lax.fori_loop(0, wide // 256, body, 0)

    def backward(src, layer):
        base = layer * 6
        acc[...] = jnp.zeros_like(acc)

        def body(b):
            s = segment(b)
            c = load(src, b) - coef[base, s]
            u = coef[base + 1, s] * c + coef[base + 2, s]
            sig = 0.5 * jnp.tanh(0.5 * u) + 0.5
            du = keep(b, load(da, b) * (sig * (1.0 + u * (1.0 - sig))))
            da[span(b), :] = flat(du)
            acc[0, s] += du[0] + du[1]
            duc = du * c
            acc[1, s] += duc[0] + duc[1]

        loop(body)
        dbeta = total(0)
        dgain = total(1) * coef[base + 3, :, 0, :]
        put(base + 4, coef[base + 4, :, 0, :] * dgain)
        put(base + 5, inv_count * dbeta)
        for k, d in enumerate((dgain, dbeta)):
            at = fc_rows(layer, k)
            sum_ref[at, :] += lax.dot_general(
                style, d, TN, precision=highest, preferred_element_type=jnp.float32
            )
            dstyle_ref[0] += lax.dot_general(
                d, w_ref[at, :].astype(jnp.float32), NT,
                precision=highest, preferred_element_type=jnp.float32,
            )
        return [jnp.sum(dgain, axis=0, keepdims=True), jnp.sum(dbeta, axis=0, keepdims=True)]

    def value_grad(src, layer, b):
        base = layer * 6
        s = segment(b)
        c = load(src, b) - coef[base, s]
        dv = coef[base + 1, s] * (load(da, b) - (c * coef[base + 4, s] + coef[base + 5, s]))
        return keep(b, dv)

    statistics(fr, 0)
    activation(fr, 0)
    spread(a3x, 0)
    on_row(0, *get_w[0], act=finish_copies)
    convolve(conv, a3x, 0)
    statistics(conv, 1)
    activation(conv, 1)
    spread(a3y, 0)
    on_row(0, *get_w[1], act=finish_copies)
    finish_copies(*get_ct)
    convolve(da, a3y, 1)
    bias = biases[4:5]
    acc[0, 0] = jnp.zeros_like(acc[0, 0])

    def finish(b):
        y = keep(b, load(da, b) + bias[None])
        res[span(b), :] = flat((load(fr, b) + y) * inv_root).astype(res.dtype)
        g = keep(b, load(ct, b) * inv_root).astype(jnp.bfloat16).astype(jnp.float32)
        hold(b, g)
        acc[0, 0] += g[0] + g[1]

    loop(finish)
    bias_sum = jnp.sum(acc[0, 0], axis=0, keepdims=True)
    put_output = start_result(0)

    dstyle_ref[...] = jnp.zeros_like(dstyle_ref)
    spread(g3, 2)
    on_row(0, *get_sums, act=finish_copies)
    weight_grad(1, a3y, g3)
    on_row(last_row, 1, act=send_sums)
    input_grad(da, g3, 1)
    rows_two = backward(conv, 1)

    def round_grad(b):
        hold(b, value_grad(conv, 1, b).astype(jnp.bfloat16).astype(jnp.float32))

    loop(round_grad)
    spread(g3, 2)
    weight_grad(0, a3x, g3)
    on_row(last_row, 0, act=send_sums)
    input_grad(da, g3, 0)
    rows_one = backward(fr, 0)

    sum_ref[bias_at : bias_at + 8, :] += jnp.concatenate(
        rows_one + rows_two + [bias_sum, jnp.zeros((3, chans), jnp.float32)], axis=0
    )
    on_row(last_row, 2, act=send_sums)
    finish_copies(*put_output)

    def frames_grad(b):
        dv = value_grad(fr, 0, b)
        res[span(b), :] = flat(load(ct, b) * inv_root + dv).astype(res.dtype)

    loop(frames_grad)
    finish_copies(*start_result(1))
    on_row(last_row, *put_sums, act=finish_copies)


def block_rows(
    n, per, first, z, lengths, seg_blocks, frames, cotangent, style, inv, weights,
    recv, from_f, from_c, to, prev, final,
):
    frames_n, width = frames.shape[1:]
    chans = width * n
    segs, style_n = style.shape[1:]
    flat_n = weights.shape[0]
    rows = len(to)
    f32 = jnp.float32

    def here(r, *_):
        return (first + r, 0, 0)

    received = [v for group in recv for v in group]
    any_space = pl.BlockSpec(memory_space=pl.ANY)
    in_specs = (
        [any_space] * 2
        + [pl.BlockSpec((1, segs, style_n), here), pl.BlockSpec((1, segs, chans), here)]
        + [any_space] * (1 + len(received) + len(prev))
    )
    out_shape = [
        jax.ShapeDtypeStruct((flat_n, chans), jnp.bfloat16 if final else f32),
        jax.ShapeDtypeStruct((rows, segs, style_n), f32),
    ]
    out_shape += [jax.ShapeDtypeStruct(frames.shape, jnp.bfloat16)] * 2
    for i in range(1 + max(i for i, _ in to)):
        size = 2 * sum(j == i for j, _ in to)
        out_shape += [jax.ShapeDtypeStruct((size, frames_n, width), jnp.bfloat16)] * (n - 1)
    out_specs = [any_space] * len(out_shape)
    out_specs[1] = pl.BlockSpec((1, segs, style_n), lambda r, *_: (r, 0, 0))
    scratch = [
        pltpu.VMEM((frames_n, chans), jnp.bfloat16),
        pltpu.VMEM((frames_n, chans), jnp.bfloat16),
        pltpu.VMEM((frames_n, chans), jnp.bfloat16),
        pltpu.VMEM((chans // 128, frames_n + 16, 128), f32),
        pltpu.VMEM((frames_n, 3 * chans), jnp.bfloat16),
        pltpu.VMEM((frames_n, 3 * chans), jnp.bfloat16),
        pltpu.VMEM((frames_n, 3 * chans), jnp.bfloat16),
        pltpu.VMEM((frames_n, chans), f32),
        pltpu.VMEM((frames_n, chans), f32),
        pltpu.VMEM((2, segs, 8, chans), f32),
        pltpu.VMEM((12, segs, 8, chans), f32),
        pltpu.VMEM((flat_n, chans), jnp.bfloat16),
        pltpu.VMEM((2, chans, 3 * chans), jnp.bfloat16),
        pltpu.VMEM((flat_n, chans), f32),
        pltpu.VMEM((flat_n if final else 16, chans), jnp.bfloat16),
        pltpu.SemaphoreType.DMA((4 * n + 16,)),
    ]
    first_prev = 3 + 5 + len(received)
    return pl.pallas_call(
        functools.partial(
            rows_kernel, n, segs, style_n, per, first, from_f, from_c, to, len(prev), final,
        ),
        grid_spec=pltpu.PrefetchScalarGridSpec(
            num_scalar_prefetch=3,
            grid=(rows,),
            in_specs=in_specs,
            out_specs=out_specs,
            scratch_shapes=scratch,
        ),
        out_shape=out_shape,
        input_output_aliases={first_prev + i: 1 + i for i in range(1, len(prev))},
        compiler_params=pltpu.CompilerParams(vmem_limit_bytes=48 << 20),
        cost_estimate=pl.CostEstimate(
            flops=int(COST * rows * 6 * 2 * 3 * frames_n * chans * chans), bytes_accessed=1000000,
            transcendentals=0,
        ),
    )(
        z, lengths, seg_blocks, frames, cotangent, style, inv, weights,
        *received, *prev,
    )


def pack_kernel(n, per, part, z_ref, i_ref, frames, conv1, conv2, fc1, fc2, biases, *refs):
    outs, mine = refs[: n - 1], refs[n - 1]
    stage, rows, sems = refs[n:]
    count = itertools.count()

    def copy(src, dst):
        c = pltpu.make_async_copy(src, dst, sems.at[next(count)])
        c.start()
        return c

    frames_n = frames.shape[1]
    at, staged = 0, []
    for ref in (conv1, conv2, fc1, fc2, biases):
        staged.append(copy(ref, stage.at[pl.ds(at, ref.shape[0]), :]))
        at += ref.shape[0]
    read = []
    for k in range(1, n):
        read.append(copy(frames.at[lax.rem(z_ref[0] + k, n) * per], rows.at[k - 1]))
    sent = []
    if at < stage.shape[0]:
        stage[at:, :] = jnp.zeros((stage.shape[0] - at, stage.shape[1]), stage.dtype)
    for c in staged:
        c.wait()
    src = stage.at[pl.ds(pl.multiple_of(i_ref[0] * part, 16), part), :]
    sent.append(copy(src, mine))
    for k in range(1, n):
        sent.append(copy(src, outs[k - 1].at[pl.ds(frames_n, part), :]))
        read[k - 1].wait()
        sent.append(copy(rows.at[k - 1], outs[k - 1].at[pl.ds(0, frames_n), :]))
    for c in sent:
        c.wait()


def pack(n, n_rows, per, z, i, frames, weights):
    frames_n, width = frames.shape[1:]
    rows = sum(v.shape[0] for v in weights)
    padded = -(-rows // (16 * n_rows)) * 16 * n_rows
    part = padded // n_rows
    any_space = pl.BlockSpec(memory_space=pl.ANY)
    return pl.pallas_call(
        functools.partial(pack_kernel, n, per, part),
        grid_spec=pltpu.PrefetchScalarGridSpec(
            num_scalar_prefetch=2,
            grid=(1,),
            in_specs=[any_space] * (1 + len(weights)),
            out_specs=[any_space] * n,
            scratch_shapes=[
                pltpu.VMEM((padded, width), jnp.bfloat16),
                pltpu.VMEM((n - 1, frames_n, width), jnp.bfloat16),
                pltpu.SemaphoreType.DMA((3 * n + len(weights),)),
            ],
        ),
        out_shape=[jax.ShapeDtypeStruct((frames_n + part, width), jnp.bfloat16)] * (n - 1)
        + [jax.ShapeDtypeStruct((part, width), jnp.bfloat16)],
        compiler_params=pltpu.CompilerParams(vmem_limit_bytes=56 << 20),
        cost_estimate=pl.CostEstimate(flops=0, bytes_accessed=6 * padded * width, transcendentals=0),
    )(z, i, frames, *weights)


def per_device(
    n,
    n_rows,
    frames,
    style_vector,
    segment_ids,
    padding,
    fc1_weight,
    fc1_bias,
    conv1_weight,
    fc2_weight,
    fc2_bias,
    conv2_weight,
    conv2_bias,
    cotangent,
):
    f32 = jnp.float32
    held, frames_n, width = frames.shape
    segs, style_n = style_vector.shape[1:]
    chans = n * width
    per = held // n
    z = lax.axis_index("ch")

    def shift(k):
        return [(i, (i + k) % n) for i in range(n)]

    def send(v, k, what):
        with jax.named_scope(what):
            return lax.ppermute(v, "ch", shift(k))

    def over_ch(v, pieces, axis):
        whole = jnp.concatenate([v] * n, axis=axis)
        size = v.shape[axis]
        for k, piece in enumerate(pieces, 1):
            at = lax.rem(z + n - k, n) * size
            whole = lax.dynamic_update_slice_in_dim(whole, piece, at, axis)
        return whole

    def after(v, others):
        return lax.optimization_barrier((v, others))[0]

    sizes = [3 * chans, 3 * chans, 2 * style_n, 2 * style_n, 2, 2, 1]
    used = sum(sizes)
    biases = jnp.concatenate(
        [fc1_bias, fc2_bias, conv2_bias[None], jnp.zeros((11, width), fc1_bias.dtype)]
    )
    shard = [v.reshape(-1, width) for v in (conv1_weight, conv2_weight, fc1_weight, fc2_weight)]
    *bundles, mine = pack(
        n, n_rows, per, z[None], lax.axis_index("rows")[None], frames, shard + [biases]
    )

    def piece(v, k, r):
        at = lax.rem(z + k, n) * per + r
        return lax.dynamic_slice_in_dim(v, at, 1, 0)[0]

    def swap(v, what):
        with jax.named_scope(what):
            return lax.all_to_all(v, "ch", 0, 0)

    def of_row(v, r):
        return v.reshape(n, per, frames_n, width)[:, r]

    def bundle(*names):
        return [
            jnp.concatenate([piece({"f": frames, "c": cotangent}[v], k, r) for v, r in names])
            for k in range(1, n)
        ]

    def fetch(what, pieces):
        return [send(v, k, what) for k, v in enumerate(pieces, 1)]

    half = per // 2
    early = [(v, r) for r in range(half) for v in "fc"]
    late = [(v, r) for r in range(half, per) for v in "fc"]
    got_a = fetch("frames_0", bundles)
    got_b = fetch("inputs_1", bundle(*early[1:]))
    got_c = fetch("inputs_2", after(bundle(*late), got_b[1]))
    mine = over_ch(mine, [v[frames_n:] for v in got_a], 1)
    mine = after(mine, got_b[1])
    weights = lax.all_gather(mine, "rows", axis=0, tiled=True)

    first = z * per
    my_ids = lax.dynamic_slice_in_dim(segment_ids, first, per, 0)
    my_pad = lax.dynamic_slice_in_dim(padding, first, per, 0)
    my_style = lax.dynamic_slice_in_dim(style_vector, first, per, 0)
    lengths = jnp.sum(my_pad, axis=1).astype(jnp.int32)
    side = jnp.full((per, 1), -1, jnp.int32)
    seg_blocks = jnp.concatenate([side, my_ids[:, ::BLOCK], side], axis=1)
    counts = jnp.sum(
        jnp.where(my_ids[:, :, None] == jnp.arange(segs, dtype=jnp.int32), my_pad[:, :, None], 0),
        axis=1,
    ).astype(f32)
    inv_count = jnp.broadcast_to(
        (1.0 / jnp.maximum(counts, 1.0))[:, :, None], (per, segs, chans)
    )

    def run(first, count, recv, from_f, from_c, to, prev):
        ids, sizes = seg_blocks[first : first + count], lengths[first : first + count]
        return block_rows(
            n, per, first, z[None], sizes, ids, frames, cotangent, my_style, inv_count, weights,
            recv, from_f, from_c, to, prev, bool(prev),
        )

    def spots(group, skip, which, rows):
        return [(group, (2 * r + which - skip) * frames_n) for r in rows]

    sums, dstyle_a, *rest = run(
        0, half, [got_a, got_b], [(0, 0)] + spots(1, 1, 0, range(1, half)),
        spots(1, 1, 1, range(half)), [(0, r) for r in range(half)], [],
    )
    own, pieces = rest[:2], after(rest[2:], got_c)
    back = [[send(v, n - k, "results_0") for k, v in enumerate(pieces, 1)]]
    others = range(per - half)
    sums, dstyle_b, *rest = run(
        half, per - half, [got_c], spots(0, 0, 0, others), spots(0, 0, 1, others),
        [(r, 0) for r in others], [sums, *own],
    )
    own, pieces = rest[:2], rest[2:]
    for r in others:
        group = pieces[r * (n - 1) : (r + 1) * (n - 1)]
        if r == 0:
            group = [group[0], *after(group[1:], back[0][2])]
        back.append([send(v, n - k, f"results_{half + r}") for k, v in enumerate(group, 1)])
    dstyles = [dstyle_a, dstyle_b]

    sums = after(sums, back[0][1:])
    sums = lax.psum_scatter(sums, "rows", scatter_dimension=0, tiled=True)
    sums = after(sums, [back[1][0], back[1][2]])
    style_grad = jnp.concatenate(dstyles, axis=0).reshape(per * segs, style_n).astype(sums.dtype)

    def share(k):
        at = lax.rem(z + k, n) * width
        return lax.dynamic_slice_in_dim(sums, at, width, 1)

    got = [send(jnp.concatenate([share(k), style_grad]), k, "sums") for k in range(1, n)]
    part = sums.shape[0]
    total = share(0).astype(f32)
    for v in got:
        total = total + v[:part].astype(f32)
    grad_style = over_ch(style_grad, [v[part:] for v in got], 0)
    grad_style = grad_style.astype(f32).reshape(style_vector.shape)
    total = after(total, [back[1][1]])
    grads = lax.all_gather(total, "rows", axis=0, tiled=True)
    splits = [sum(sizes[: i + 1]) for i in range(len(sizes))]
    g1, g2, gf1, gf2, gb1, gb2, gb = [
        grads[end - size : end] for size, end in zip(sizes, splits)
    ]
    grads = [
        gf1.reshape(fc1_weight.shape),
        gb1,
        g1.reshape(conv1_weight.shape),
        gf2.reshape(fc2_weight.shape),
        gb2,
        g2.reshape(conv2_weight.shape),
        gb[0],
    ]

    results = [v.reshape(n, per, frames_n, width) for v in own]
    for r in range(per):
        if r == per - 1:
            grads, results = lax.optimization_barrier((grads, results))
        group, at = (0, r) if r < half else (r - half + 1, 0)
        for which in range(2):
            for k, v in enumerate(back[group], 1):
                results[which] = lax.dynamic_update_slice(
                    results[which], v[None, None, 2 * at + which], (lax.rem(z + k, n), r, 0, 0)
                )
    output, grad_frames = [v.reshape(frames.shape) for v in results]
    return (output, grad_frames, grad_style, *grads)


def solution(mesh):
    return jax.shard_map(
        functools.partial(per_device, mesh.shape["ch"], mesh.shape["rows"]),
        mesh=mesh,
        in_specs=(
            P("rows", None, "ch"),
            P("rows", None, None),
            P("rows", None),
            P("rows", None),
            P(None, None, "ch"),
            P(None, "ch"),
            P(None, None, "ch"),
            P(None, None, "ch"),
            P(None, "ch"),
            P(None, None, "ch"),
            P("ch"),
            P("rows", None, "ch"),
        ),
        out_specs=(
            P("rows", None, "ch"),
            P("rows", None, "ch"),
            P("rows", None, None),
            P(None, None, "ch"),
            P(None, "ch"),
            P(None, None, "ch"),
            P(None, None, "ch"),
            P(None, "ch"),
            P(None, None, "ch"),
            P("ch"),
        ),
        check_vma=False,
    )
```

```python
import functools
import itertools
import math

import jax
import jax.numpy as jnp
from jax import lax
from jax.experimental import pallas as pl
from jax.experimental.pallas import tpu as pltpu
from jax.sharding import PartitionSpec as P

var_floor = 0.1
inv_root = math.sqrt(0.5)
highest = lax.Precision.HIGHEST
COST = 0.5
BLOCK = 16
NT = (((1,), (1,)), ((), ()))
TN = (((0,), (0,)), ((), ()))


def rows_kernel(
    n, segs, style_n, per, first, from_f, from_c, to, has_prev, final, z_ref, len_ref, seg_ref, *refs
):
    f_own, c_own, style_ref, inv_ref, w_hbm = refs[:5]
    refs = refs[5:]
    n_recv = 1 + max(i for i, _ in from_f + from_c)
    recv, refs = refs[: n_recv * (n - 1)], refs[n_recv * (n - 1) :]
    prev, refs = refs[:has_prev], refs[has_prev:]
    sum_hbm, dstyle_ref, o_own, g_own = refs[:4]
    outs = refs[4:-16]
    fr, ct, res, sh, a3x, a3y, g3, conv, da, acc, coef, w_ref, wt_ref, sum_ref = refs[-16:-2]
    round_ref, sems = refs[-2:]

    row = pl.program_id(0)
    last_row = len(from_f) - 1
    z = z_ref[0]
    length = len_ref[row]
    frames, chans = fr.shape
    width = chans // n
    blocks = frames // BLOCK
    wide = 3 * chans
    fc_at = 2 * wide
    bias_at = fc_at + 4 * style_n
    row_iota = (
        lax.broadcasted_iota(jnp.int32, (2, 8, chans), 0) * 8
        + lax.broadcasted_iota(jnp.int32, (2, 8, chans), 1)
    )
    edge = lax.broadcasted_iota(jnp.int32, (8, 128), 0)

    def lanes(k):
        return pl.ds(pl.multiple_of(lax.rem(z + n - k, n) * width, width), width)

    def span(b):
        return pl.ds(pl.multiple_of(b * BLOCK, BLOCK), BLOCK)

    def segment(b):
        return seg_ref[row, b + 1]

    def load(ref, b):
        return ref[span(b), :].astype(jnp.float32).reshape(2, 8, chans)

    def flat(v):
        return v.reshape(BLOCK, chans)

    def keep(b, v):
        return jnp.where(row_iota < length - b * BLOCK, v, 0.0)

    def loop(body, unroll=4):
        def step(i, carry):
            for j in range(unroll):
                body(i * unroll + j)
            return carry

        lax.fori_loop(0, blocks // unroll, step, 0)

    def total(slot):
        return jnp.sum(acc[slot], axis=1)

    def put(slot, v):
        coef[slot] = jnp.broadcast_to(v[:, None, :], (segs, 8, chans))

    def fc_rows(layer, k):
        at = fc_at + (2 * layer + k) * style_n
        return slice(at, at + style_n)

    count = itertools.count()

    def copy(src, dst):
        return pltpu.make_async_copy(src, dst, sems.at[next(count)])

    def begin(*copies):
        for c in copies:
            c.start()

    def finish_copies(*copies):
        for c in copies:
            c.wait()

    def pieces(own, place, at_row, dst):
        which, at = place
        yield copy(own.at[z * per + first + at_row], dst.at[:, lanes(0)])
        for k in range(1, n):
            ref = recv[which * (n - 1) + k - 1]
            yield copy(ref.at[pl.ds(at, frames), :], dst.at[:, lanes(k)])

    def weight_copies(layer):
        rows = pl.ds(layer * wide, wide)
        yield copy(w_hbm.at[rows, :], w_ref.at[rows, :])
        for k in range(3):
            rows = pl.ds(layer * wide + k * chans, chans)
            yield copy(w_hbm.at[rows, :], wt_ref.at[layer, :, k * chans : (k + 1) * chans])

    tail_rows = pl.ds(fc_at, w_ref.shape[0] - fc_at)
    layer_rows = [pl.ds(layer * wide, wide) for layer in range(2)]
    get_tail = copy(w_hbm.at[tail_rows, :], w_ref.at[tail_rows, :])
    get_w = [list(weight_copies(layer)) for layer in range(2)]
    get_sums = []
    if has_prev:
        get_sums = [copy(prev[0].at[r, :], sum_ref.at[r, :]) for r in (*layer_rows, tail_rows)]
    sum_out = round_ref if final else sum_ref
    put_sums = [copy(sum_out.at[r, :], sum_hbm.at[r, :]) for r in (*layer_rows, tail_rows)]

    def send_sums(part):
        rows = (*layer_rows, tail_rows)[part]
        if final:

            def body(i, carry):
                at = pl.ds(pl.multiple_of(rows.start + i * 128, 16), 128)
                round_ref[at, :] = sum_ref[at, :].astype(round_ref.dtype)
                return carry

            lax.fori_loop(0, rows.size // 128, body, 0)
        begin(put_sums[part])

    mark = next(count)
    get = []
    for i in range(last_row + 1):
        count = itertools.count(mark)
        get_fr = list(pieces(f_own, from_f[i], i, fr))
        get_ct = list(pieces(c_own, from_c[i], i, ct))
        pl.when(row == i)(functools.partial(begin, *get_fr, *get_ct))

    @pl.when(row == 0)
    def _():
        begin(get_tail, *get_w[0], *get_w[1], *get_sums[::-1])
        if not has_prev:
            sum_ref[...] = jnp.zeros_like(sum_ref)

    mark_out = next(count)

    def put_result(which, at_row):
        yield copy(res.at[:, lanes(0)], (o_own, g_own)[which].at[z * per + first + at_row])
        array, at = to[at_row]
        for k in range(1, n):
            dst = outs[array * (n - 1) + k - 1].at[2 * at + which]
            yield copy(res.at[:, lanes(k)], dst)

    def start_result(which):
        nonlocal count
        for i in range(last_row + 1):
            count = itertools.count(mark_out + n * which)
            copies = list(put_result(which, i))
            pl.when(row == i)(functools.partial(begin, *copies))
        return copies

    def on_row(i, *copies, act):
        pl.when(row == i)(functools.partial(act, *copies))

    for j in range(chans // 128):
        sh[j, 0:8, :] = jnp.zeros((8, 128), jnp.float32)
        sh[j, 8 + frames :, :] = jnp.zeros((8, 128), jnp.float32)

    inv_count = inv_ref[0]
    style = style_ref[0].astype(jnp.float32)
    finish_copies(*get_fr)
    on_row(0, get_tail, act=finish_copies)
    biases = w_ref[bias_at : bias_at + BLOCK, :].astype(jnp.float32)

    def project(layer, k):
        proj = jnp.dot(
            style, w_ref[fc_rows(layer, k), :].astype(jnp.float32),
            precision=highest, preferred_element_type=jnp.float32,
        )
        return proj + biases[2 * layer + k : 2 * layer + k + 1]

    def hold(b, v):
        at = pl.ds(pl.multiple_of(b * BLOCK + 8, 8), BLOCK)
        v = flat(v)
        for j in range(chans // 128):
            sh[j, at, :] = v[:, j * 128 : (j + 1) * 128]

    def statistics(src, layer):
        base = layer * 6
        acc[0] = jnp.zeros_like(acc[0])

        def add_values(b):
            v = keep(b, load(src, b))
            acc[0, segment(b)] += v[0] + v[1]

        loop(add_values)
        put(base, total(0) * inv_count)
        acc[0] = jnp.zeros_like(acc[0])

        def add_squares(b):
            s = segment(b)
            c = keep(b, load(src, b) - coef[base, s])
            c = c * c
            acc[0, s] += c[0] + c[1]

        loop(add_squares)
        var = total(0) * inv_count
        rstd = lax.rsqrt(jnp.maximum(var, var_floor))
        put(base + 1, (1.0 + project(layer, 0)) * rstd)
        put(base + 2, project(layer, 1))
        put(base + 3, rstd)
        put(base + 4, jnp.where(var > var_floor, rstd, 0.0) * inv_count)

    def activation(src, layer):
        base = layer * 6

        def body(b):
            s = segment(b)
            u = coef[base + 1, s] * (load(src, b) - coef[base, s]) + coef[base + 2, s]
            hold(b, keep(b, u * (0.5 * jnp.tanh(0.5 * u) + 0.5)))

        loop(body)

    def spread(dst, first):
        last = 2 - first

        def body(b):
            s = segment(b)
            from_row = jnp.where(seg_ref[row, b] == s, 0, 1)
            to_row = jnp.where(seg_ref[row, b + 2] == s, 8, 7)
            for j in range(chans // 128):

                def part(off):
                    return sh[j, pl.ds(b * BLOCK + off, 8), :]

                def store(tap, low, high):
                    at = tap * chans + j * 128
                    v = jnp.concatenate([low, high], axis=0)
                    dst[span(b), at : at + 128] = v.astype(dst.dtype)

                store(first, jnp.where(edge >= from_row, part(7), 0.0), part(15))
                store(1, part(8), part(16))
                store(last, part(9), jnp.where(edge < to_row, part(17), 0.0))

        loop(body)

    tile = min(frames, 1024)

    def convolve(dst, src, layer):
        def body(i, carry):
            at = pl.ds(pl.multiple_of(i * tile, tile), tile)
            dst[at, :] = jnp.dot(
                src[at, :], w_ref[layer * wide : (layer + 1) * wide, :],
                preferred_element_type=jnp.float32,
            )
            return carry

        lax.fori_loop(0, frames // tile, body, 0)

    def input_grad(dst, src, layer):
        def body(i, carry):
            at = pl.ds(pl.multiple_of(i * tile, tile), tile)
            dst[at, :] = lax.dot_general(
                src[at, :], wt_ref[layer], NT, preferred_element_type=jnp.float32
            )
            return carry

        lax.fori_loop(0, frames // tile, body, 0)

    def weight_grad(layer, kept, grads):
        def body(i, carry):
            at = pl.ds(pl.multiple_of(i * 256, 256), 256)
            to = pl.ds(pl.multiple_of(layer * wide + i * 256, 256), 256)
            sum_ref[to, :] += lax.dot_general(
                kept[:, at], grads[:, chans : 2 * chans], TN, preferred_element_type=jnp.float32
            )
            return carry

        lax.fori_loop(0, wide // 256, body, 0)

    def backward(src, layer):
        base = layer * 6
        acc[...] = jnp.zeros_like(acc)

        def body(b):
            s = segment(b)
            c = load(src, b) - coef[base, s]
            u = coef[base + 1, s] * c + coef[base + 2, s]
            sig = 0.5 * jnp.tanh(0.5 * u) + 0.5
            du = keep(b, load(da, b) * (sig * (1.0 + u * (1.0 - sig))))
            da[span(b), :] = flat(du)
            acc[0, s] += du[0] + du[1]
            duc = du * c
            acc[1, s] += duc[0] + duc[1]

        loop(body)
        dbeta = total(0)
        dgain = total(1) * coef[base + 3, :, 0, :]
        put(base + 4, coef[base + 4, :, 0, :] * dgain)
        put(base + 5, inv_count * dbeta)
        for k, d in enumerate((dgain, dbeta)):
            at = fc_rows(layer, k)
            sum_ref[at, :] += lax.dot_general(
                style, d, TN, precision=highest, preferred_element_type=jnp.float32
            )
            dstyle_ref[0] += lax.dot_general(
                d, w_ref[at, :].astype(jnp.float32), NT,
                precision=highest, preferred_element_type=jnp.float32,
            )
        return [jnp.sum(dgain, axis=0, keepdims=True), jnp.sum(dbeta, axis=0, keepdims=True)]

    def value_grad(src, layer, b):
        base = layer * 6
        s = segment(b)
        c = load(src, b) - coef[base, s]
        dv = coef[base + 1, s] * (load(da, b) - (c * coef[base + 4, s] + coef[base + 5, s]))
        return keep(b, dv)

    statistics(fr, 0)
    activation(fr, 0)
    spread(a3x, 0)
    on_row(0, *get_w[0], act=finish_copies)
    convolve(conv, a3x, 0)
    statistics(conv, 1)
    activation(conv, 1)
    spread(a3y, 0)
    on_row(0, *get_w[1], act=finish_copies)
    finish_copies(*get_ct)
    convolve(da, a3y, 1)
    bias = biases[4:5]
    acc[0, 0] = jnp.zeros_like(acc[0, 0])

    def finish(b):
        y = keep(b, load(da, b) + bias[None])
        res[span(b), :] = flat((load(fr, b) + y) * inv_root).astype(res.dtype)
        g = keep(b, load(ct, b) * inv_root).astype(jnp.bfloat16).astype(jnp.float32)
        hold(b, g)
        acc[0, 0] += g[0] + g[1]

    loop(finish)
    bias_sum = jnp.sum(acc[0, 0], axis=0, keepdims=True)
    put_output = start_result(0)

    dstyle_ref[...] = jnp.zeros_like(dstyle_ref)
    spread(g3, 2)
    on_row(0, *get_sums, act=finish_copies)
    weight_grad(1, a3y, g3)
    on_row(last_row, 1, act=send_sums)
    input_grad(da, g3, 1)
    rows_two = backward(conv, 1)

    def round_grad(b):
        hold(b, value_grad(conv, 1, b).astype(jnp.bfloat16).astype(jnp.float32))

    loop(round_grad)
    spread(g3, 2)
    weight_grad(0, a3x, g3)
    on_row(last_row, 0, act=send_sums)
    input_grad(da, g3, 0)
    rows_one = backward(fr, 0)

    sum_ref[bias_at : bias_at + 8, :] += jnp.concatenate(
        rows_one + rows_two + [bias_sum, jnp.zeros((3, chans), jnp.float32)], axis=0
    )
    on_row(last_row, 2, act=send_sums)
    finish_copies(*put_output)

    def frames_grad(b):
        dv = value_grad(fr, 0, b)
        res[span(b), :] = flat(load(ct, b) * inv_root + dv).astype(res.dtype)

    loop(frames_grad)
    finish_copies(*start_result(1))
    on_row(last_row, *put_sums, act=finish_copies)


def block_rows(
    n, per, first, z, lengths, seg_blocks, frames, cotangent, style, inv, weights,
    recv, from_f, from_c, to, prev, final,
):
    frames_n, width = frames.shape[1:]
    chans = width * n
    segs, style_n = style.shape[1:]
    flat_n = weights.shape[0]
    rows = len(to)
    f32 = jnp.float32

    def here(r, *_):
        return (first + r, 0, 0)

    received = [v for group in recv for v in group]
    any_space = pl.BlockSpec(memory_space=pl.ANY)
    in_specs = (
        [any_space] * 2
        + [pl.BlockSpec((1, segs, style_n), here), pl.BlockSpec((1, segs, chans), here)]
        + [any_space] * (1 + len(received) + len(prev))
    )
    out_shape = [
        jax.ShapeDtypeStruct((flat_n, chans), jnp.bfloat16 if final else f32),
        jax.ShapeDtypeStruct((rows, segs, style_n), f32),
    ]
    out_shape += [jax.ShapeDtypeStruct(frames.shape, jnp.bfloat16)] * 2
    for i in range(1 + max(i for i, _ in to)):
        size = 2 * sum(j == i for j, _ in to)
        out_shape += [jax.ShapeDtypeStruct((size, frames_n, width), jnp.bfloat16)] * (n - 1)
    out_specs = [any_space] * len(out_shape)
    out_specs[1] = pl.BlockSpec((1, segs, style_n), lambda r, *_: (r, 0, 0))
    scratch = [
        pltpu.VMEM((frames_n, chans), jnp.bfloat16),
        pltpu.VMEM((frames_n, chans), jnp.bfloat16),
        pltpu.VMEM((frames_n, chans), jnp.bfloat16),
        pltpu.VMEM((chans // 128, frames_n + 16, 128), f32),
        pltpu.VMEM((frames_n, 3 * chans), jnp.bfloat16),
        pltpu.VMEM((frames_n, 3 * chans), jnp.bfloat16),
        pltpu.VMEM((frames_n, 3 * chans), jnp.bfloat16),
        pltpu.VMEM((frames_n, chans), f32),
        pltpu.VMEM((frames_n, chans), f32),
        pltpu.VMEM((2, segs, 8, chans), f32),
        pltpu.VMEM((12, segs, 8, chans), f32),
        pltpu.VMEM((flat_n, chans), jnp.bfloat16),
        pltpu.VMEM((2, chans, 3 * chans), jnp.bfloat16),
        pltpu.VMEM((flat_n, chans), f32),
        pltpu.VMEM((flat_n if final else 16, chans), jnp.bfloat16),
        pltpu.SemaphoreType.DMA((4 * n + 16,)),
    ]
    first_prev = 3 + 5 + len(received)
    return pl.pallas_call(
        functools.partial(
            rows_kernel, n, segs, style_n, per, first, from_f, from_c, to, len(prev), final,
        ),
        grid_spec=pltpu.PrefetchScalarGridSpec(
            num_scalar_prefetch=3,
            grid=(rows,),
            in_specs=in_specs,
            out_specs=out_specs,
            scratch_shapes=scratch,
        ),
        out_shape=out_shape,
        input_output_aliases={first_prev + i: 1 + i for i in range(1, len(prev))},
        compiler_params=pltpu.CompilerParams(vmem_limit_bytes=48 << 20),
        cost_estimate=pl.CostEstimate(
            flops=int(COST * rows * 6 * 2 * 3 * frames_n * chans * chans), bytes_accessed=1000000,
            transcendentals=0,
        ),
    )(
        z, lengths, seg_blocks, frames, cotangent, style, inv, weights,
        *received, *prev,
    )


def pack_kernel(n, per, part, z_ref, i_ref, frames, conv1, conv2, fc1, fc2, biases, *refs):
    outs, mine = refs[: n - 1], refs[n - 1]
    stage, rows, sems = refs[n:]
    count = itertools.count()

    def copy(src, dst):
        c = pltpu.make_async_copy(src, dst, sems.at[next(count)])
        c.start()
        return c

    frames_n = frames.shape[1]
    at, staged = 0, []
    for ref in (conv1, conv2, fc1, fc2, biases):
        staged.append(copy(ref, stage.at[pl.ds(at, ref.shape[0]), :]))
        at += ref.shape[0]
    read = []
    for k in range(1, n):
        read.append(copy(frames.at[lax.rem(z_ref[0] + k, n) * per], rows.at[k - 1]))
    sent = []
    if at < stage.shape[0]:
        stage[at:, :] = jnp.zeros((stage.shape[0] - at, stage.shape[1]), stage.dtype)
    for c in staged:
        c.wait()
    src = stage.at[pl.ds(pl.multiple_of(i_ref[0] * part, 16), part), :]
    sent.append(copy(src, mine))
    for k in range(1, n):
        sent.append(copy(src, outs[k - 1].at[pl.ds(frames_n, part), :]))
        read[k - 1].wait()
        sent.append(copy(rows.at[k - 1], outs[k - 1].at[pl.ds(0, frames_n), :]))
    for c in sent:
        c.wait()


def pack(n, n_rows, per, z, i, frames, weights):
    frames_n, width = frames.shape[1:]
    rows = sum(v.shape[0] for v in weights)
    padded = -(-rows // (16 * n_rows)) * 16 * n_rows
    part = padded // n_rows
    any_space = pl.BlockSpec(memory_space=pl.ANY)
    return pl.pallas_call(
        functools.partial(pack_kernel, n, per, part),
        grid_spec=pltpu.PrefetchScalarGridSpec(
            num_scalar_prefetch=2,
            grid=(1,),
            in_specs=[any_space] * (1 + len(weights)),
            out_specs=[any_space] * n,
            scratch_shapes=[
                pltpu.VMEM((padded, width), jnp.bfloat16),
                pltpu.VMEM((n - 1, frames_n, width), jnp.bfloat16),
                pltpu.SemaphoreType.DMA((3 * n + len(weights),)),
            ],
        ),
        out_shape=[jax.ShapeDtypeStruct((frames_n + part, width), jnp.bfloat16)] * (n - 1)
        + [jax.ShapeDtypeStruct((part, width), jnp.bfloat16)],
        compiler_params=pltpu.CompilerParams(vmem_limit_bytes=56 << 20),
        cost_estimate=pl.CostEstimate(flops=0, bytes_accessed=6 * padded * width, transcendentals=0),
    )(z, i, frames, *weights)


def bundle_kernel(n, per, names, z_ref, frames, cotangent, *refs):
    outs, stage, sems = refs[: n - 1], refs[n - 1], refs[n]
    frames_n = frames.shape[1]
    count = itertools.count()

    def copy(src, dst):
        c = pltpu.make_async_copy(src, dst, sems.at[next(count)])
        c.start()
        return c

    read = []
    for k in range(1, n):
        for i, (v, r) in enumerate(names):
            src = (frames if v == "f" else cotangent).at[lax.rem(z_ref[0] + k, n) * per + r]
            at = pl.ds(i * frames_n, frames_n)
            read.append((k, at, copy(src, stage.at[k - 1, at, :])))
    sent = []
    for k, at, c in read:
        c.wait()
        sent.append(copy(stage.at[k - 1, at, :], outs[k - 1].at[at, :]))
    for c in sent:
        c.wait()


def bundle_rows(n, per, names, z, frames, cotangent):
    frames_n, width = frames.shape[1:]
    size = len(names) * frames_n
    any_space = pl.BlockSpec(memory_space=pl.ANY)
    return pl.pallas_call(
        functools.partial(bundle_kernel, n, per, names),
        grid_spec=pltpu.PrefetchScalarGridSpec(
            num_scalar_prefetch=1,
            grid=(1,),
            in_specs=[any_space] * 2,
            out_specs=[any_space] * (n - 1),
            scratch_shapes=[
                pltpu.VMEM((n - 1, size, width), jnp.bfloat16),
                pltpu.SemaphoreType.DMA((2 * (n - 1) * len(names),)),
            ],
        ),
        out_shape=[jax.ShapeDtypeStruct((size, width), jnp.bfloat16)] * (n - 1),
        compiler_params=pltpu.CompilerParams(vmem_limit_bytes=56 << 20),
        cost_estimate=pl.CostEstimate(
            flops=0, bytes_accessed=4 * (n - 1) * size * width, transcendentals=0
        ),
    )(z, frames, cotangent)


def per_device(
    n,
    n_rows,
    frames,
    style_vector,
    segment_ids,
    padding,
    fc1_weight,
    fc1_bias,
    conv1_weight,
    fc2_weight,
    fc2_bias,
    conv2_weight,
    conv2_bias,
    cotangent,
):
    f32 = jnp.float32
    held, frames_n, width = frames.shape
    segs, style_n = style_vector.shape[1:]
    chans = n * width
    per = held // n
    z = lax.axis_index("ch")

    def shift(k):
        return [(i, (i + k) % n) for i in range(n)]

    def send(v, k, what):
        with jax.named_scope(what):
            return lax.ppermute(v, "ch", shift(k))

    def over_ch(v, pieces, axis):
        whole = jnp.concatenate([v] * n, axis=axis)
        size = v.shape[axis]
        for k, piece in enumerate(pieces, 1):
            at = lax.rem(z + n - k, n) * size
            whole = lax.dynamic_update_slice_in_dim(whole, piece, at, axis)
        return whole

    def after(v, others):
        return lax.optimization_barrier((v, others))[0]

    sizes = [3 * chans, 3 * chans, 2 * style_n, 2 * style_n, 2, 2, 1]
    used = sum(sizes)
    biases = jnp.concatenate(
        [fc1_bias, fc2_bias, conv2_bias[None], jnp.zeros((11, width), fc1_bias.dtype)]
    )
    shard = [v.reshape(-1, width) for v in (conv1_weight, conv2_weight, fc1_weight, fc2_weight)]
    *bundles, mine = pack(
        n, n_rows, per, z[None], lax.axis_index("rows")[None], frames, shard + [biases]
    )

    def piece(v, k, r):
        at = lax.rem(z + k, n) * per + r
        return lax.dynamic_slice_in_dim(v, at, 1, 0)[0]

    def swap(v, what):
        with jax.named_scope(what):
            return lax.all_to_all(v, "ch", 0, 0)

    def of_row(v, r):
        return v.reshape(n, per, frames_n, width)[:, r]

    def bundle(*names):
        return bundle_rows(n, per, names, z[None], frames, cotangent)

    def fetch(what, pieces):
        return [send(v, k, what) for k, v in enumerate(pieces, 1)]

    half = per // 2
    early = [(v, r) for r in range(half) for v in "fc"]
    late = [(v, r) for r in range(half, per) for v in "fc"]
    got_a = fetch("frames_0", bundles)
    got_b = fetch("inputs_1", bundle(*early[1:]))
    got_c = fetch("inputs_2", after(bundle(*late), got_b[1]))
    mine = over_ch(mine, [v[frames_n:] for v in got_a], 1)
    mine = after(mine, got_b[1])
    weights = lax.all_gather(mine, "rows", axis=0, tiled=True)

    first = z * per
    my_ids = lax.dynamic_slice_in_dim(segment_ids, first, per, 0)
    my_pad = lax.dynamic_slice_in_dim(padding, first, per, 0)
    my_style = lax.dynamic_slice_in_dim(style_vector, first, per, 0)
    lengths = jnp.sum(my_pad, axis=1).astype(jnp.int32)
    side = jnp.full((per, 1), -1, jnp.int32)
    seg_blocks = jnp.concatenate([side, my_ids[:, ::BLOCK], side], axis=1)
    counts = jnp.sum(
        jnp.where(my_ids[:, :, None] == jnp.arange(segs, dtype=jnp.int32), my_pad[:, :, None], 0),
        axis=1,
    ).astype(f32)
    inv_count = jnp.broadcast_to(
        (1.0 / jnp.maximum(counts, 1.0))[:, :, None], (per, segs, chans)
    )

    def run(first, count, recv, from_f, from_c, to, prev):
        ids, sizes = seg_blocks[first : first + count], lengths[first : first + count]
        return block_rows(
            n, per, first, z[None], sizes, ids, frames, cotangent, my_style, inv_count, weights,
            recv, from_f, from_c, to, prev, bool(prev),
        )

    def spots(group, skip, which, rows):
        return [(group, (2 * r + which - skip) * frames_n) for r in rows]

    sums, dstyle_a, *rest = run(
        0, half, [got_a, got_b], [(0, 0)] + spots(1, 1, 0, range(1, half)),
        spots(1, 1, 1, range(half)), [(0, r) for r in range(half)], [],
    )
    own, pieces = rest[:2], after(rest[2:], got_c)
    back = [[send(v, n - k, "results_0") for k, v in enumerate(pieces, 1)]]
    others = range(per - half)
    sums, dstyle_b, *rest = run(
        half, per - half, [got_c], spots(0, 0, 0, others), spots(0, 0, 1, others),
        [(r, 0) for r in others], [sums, *own],
    )
    own, pieces = rest[:2], rest[2:]
    for r in others:
        group = pieces[r * (n - 1) : (r + 1) * (n - 1)]
        if r == 0:
            group = [group[0], *after(group[1:], back[0][2])]
        back.append([send(v, n - k, f"results_{half + r}") for k, v in enumerate(group, 1)])
    dstyles = [dstyle_a, dstyle_b]

    sums = after(sums, back[0][1:])
    sums = lax.psum_scatter(sums, "rows", scatter_dimension=0, tiled=True)
    sums = after(sums, [back[1][0], back[1][2]])
    style_grad = jnp.concatenate(dstyles, axis=0).reshape(per * segs, style_n).astype(sums.dtype)

    def share(k):
        at = lax.rem(z + k, n) * width
        return lax.dynamic_slice_in_dim(sums, at, width, 1)

    got = [send(jnp.concatenate([share(k), style_grad]), k, "sums") for k in range(1, n)]
    part = sums.shape[0]
    total = share(0).astype(f32)
    for v in got:
        total = total + v[:part].astype(f32)
    grad_style = over_ch(style_grad, [v[part:] for v in got], 0)
    grad_style = grad_style.astype(f32).reshape(style_vector.shape)
    total = after(total, [back[1][1]])
    grads = lax.all_gather(total, "rows", axis=0, tiled=True)
    splits = [sum(sizes[: i + 1]) for i in range(len(sizes))]
    g1, g2, gf1, gf2, gb1, gb2, gb = [
        grads[end - size : end] for size, end in zip(sizes, splits)
    ]
    grads = [
        gf1.reshape(fc1_weight.shape),
        gb1,
        g1.reshape(conv1_weight.shape),
        gf2.reshape(fc2_weight.shape),
        gb2,
        g2.reshape(conv2_weight.shape),
        gb[0],
    ]

    results = [v.reshape(n, per, frames_n, width) for v in own]
    for r in range(per):
        if r == per - 1:
            grads, results = lax.optimization_barrier((grads, results))
        group, at = (0, r) if r < half else (r - half + 1, 0)
        for which in range(2):
            for k, v in enumerate(back[group], 1):
                results[which] = lax.dynamic_update_slice(
                    results[which], v[None, None, 2 * at + which], (lax.rem(z + k, n), r, 0, 0)
                )
    output, grad_frames = [v.reshape(frames.shape) for v in results]
    return (output, grad_frames, grad_style, *grads)


def solution(mesh):
    return jax.shard_map(
        functools.partial(per_device, mesh.shape["ch"], mesh.shape["rows"]),
        mesh=mesh,
        in_specs=(
            P("rows", None, "ch"),
            P("rows", None, None),
            P("rows", None),
            P("rows", None),
            P(None, None, "ch"),
            P(None, "ch"),
            P(None, None, "ch"),
            P(None, None, "ch"),
            P(None, "ch"),
            P(None, None, "ch"),
            P("ch"),
            P("rows", None, "ch"),
        ),
        out_specs=(
            P("rows", None, "ch"),
            P("rows", None, "ch"),
            P("rows", None, None),
            P(None, None, "ch"),
            P(None, "ch"),
            P(None, None, "ch"),
            P(None, None, "ch"),
            P(None, "ch"),
            P(None, None, "ch"),
            P("ch"),
        ),
        check_vma=False,
    )
```

```python
import functools
import itertools
import math

import jax
import jax.numpy as jnp
from jax import lax
from jax.experimental import pallas as pl
from jax.experimental.pallas import tpu as pltpu
from jax.sharding import PartitionSpec as P

var_floor = 0.1
inv_root = math.sqrt(0.5)
highest = lax.Precision.HIGHEST
COST = 0.5
BLOCK = 16
NT = (((1,), (1,)), ((), ()))
TN = (((0,), (0,)), ((), ()))


def rows_kernel(
    n, segs, style_n, per, first, from_f, from_c, to, has_prev, final, z_ref, len_ref, seg_ref, *refs
):
    f_own, c_own, style_ref, inv_ref, w_hbm = refs[:5]
    refs = refs[5:]
    n_recv = 1 + max(i for i, _ in from_f + from_c)
    recv, refs = refs[: n_recv * (n - 1)], refs[n_recv * (n - 1) :]
    prev, refs = refs[:has_prev], refs[has_prev:]
    sum_hbm, dstyle_ref, o_own, g_own = refs[:4]
    outs = refs[4:-16]
    fr, ct, res, sh, a3x, a3y, g3, conv, da, acc, coef, w_ref, wt_ref, sum_ref = refs[-16:-2]
    round_ref, sems = refs[-2:]

    row = pl.program_id(0)
    last_row = len(from_f) - 1
    z = z_ref[0]
    length = len_ref[row]
    frames, chans = fr.shape
    width = chans // n
    blocks = frames // BLOCK
    wide = 3 * chans
    fc_at = 2 * wide
    bias_at = fc_at + 4 * style_n
    row_iota = (
        lax.broadcasted_iota(jnp.int32, (2, 8, chans), 0) * 8
        + lax.broadcasted_iota(jnp.int32, (2, 8, chans), 1)
    )
    edge = lax.broadcasted_iota(jnp.int32, (8, 128), 0)

    def lanes(k):
        return pl.ds(pl.multiple_of(lax.rem(z + n - k, n) * width, width), width)

    def span(b):
        return pl.ds(pl.multiple_of(b * BLOCK, BLOCK), BLOCK)

    def segment(b):
        return seg_ref[row, b + 1]

    def load(ref, b):
        return ref[span(b), :].astype(jnp.float32).reshape(2, 8, chans)

    def flat(v):
        return v.reshape(BLOCK, chans)

    def keep(b, v):
        return jnp.where(row_iota < length - b * BLOCK, v, 0.0)

    def loop(body, unroll=4):
        def step(i, carry):
            for j in range(unroll):
                body(i * unroll + j)
            return carry

        lax.fori_loop(0, blocks // unroll, step, 0)

    def total(slot):
        return jnp.sum(acc[slot], axis=1)

    def put(slot, v):
        coef[slot] = jnp.broadcast_to(v[:, None, :], (segs, 8, chans))

    def fc_rows(layer, k):
        at = fc_at + (2 * layer + k) * style_n
        return slice(at, at + style_n)

    count = itertools.count()

    def copy(src, dst):
        return pltpu.make_async_copy(src, dst, sems.at[next(count)])

    def begin(*copies):
        for c in copies:
            c.start()

    def finish_copies(*copies):
        for c in copies:
            c.wait()

    def pieces(own, place, at_row, dst):
        which, at = place
        yield copy(own.at[z * per + first + at_row], dst.at[:, lanes(0)])
        for k in range(1, n):
            ref = recv[which * (n - 1) + k - 1]
            yield copy(ref.at[pl.ds(at, frames), :], dst.at[:, lanes(k)])

    def weight_copies(layer):
        rows = pl.ds(layer * wide, wide)
        yield copy(w_hbm.at[rows, :], w_ref.at[rows, :])
        for k in range(3):
            rows = pl.ds(layer * wide + k * chans, chans)
            yield copy(w_hbm.at[rows, :], wt_ref.at[layer, :, k * chans : (k + 1) * chans])

    tail_rows = pl.ds(fc_at, w_ref.shape[0] - fc_at)
    layer_rows = [pl.ds(layer * wide, wide) for layer in range(2)]
    get_tail = copy(w_hbm.at[tail_rows, :], w_ref.at[tail_rows, :])
    get_w = [list(weight_copies(layer)) for layer in range(2)]
    get_sums = []
    if has_prev:
        get_sums = [copy(prev[0].at[r, :], sum_ref.at[r, :]) for r in (*layer_rows, tail_rows)]
    sum_out = round_ref if final else sum_ref
    put_sums = [copy(sum_out.at[r, :], sum_hbm.at[r, :]) for r in (*layer_rows, tail_rows)]

    def send_sums(part):
        rows = (*layer_rows, tail_rows)[part]
        if final:

            def body(i, carry):
                at = pl.ds(pl.multiple_of(rows.start + i * 128, 16), 128)
                round_ref[at, :] = sum_ref[at, :].astype(round_ref.dtype)
                return carry

            lax.fori_loop(0, rows.size // 128, body, 0)
        begin(put_sums[part])

    mark = next(count)
    get = []
    for i in range(last_row + 1):
        count = itertools.count(mark)
        get_fr = list(pieces(f_own, from_f[i], i, fr))
        get_ct = list(pieces(c_own, from_c[i], i, ct))
        pl.when(row == i)(functools.partial(begin, *get_fr, *get_ct))

    @pl.when(row == 0)
    def _():
        begin(get_tail, *get_w[0], *get_w[1], *get_sums[::-1])
        if not has_prev:
            sum_ref[...] = jnp.zeros_like(sum_ref)

    mark_out = next(count)

    def put_result(which, at_row):
        yield copy(res.at[:, lanes(0)], (o_own, g_own)[which].at[z * per + first + at_row])
        array, at = to[at_row]
        for k in range(1, n):
            dst = outs[array * (n - 1) + k - 1].at[2 * at + which]
            yield copy(res.at[:, lanes(k)], dst)

    def start_result(which):
        nonlocal count
        for i in range(last_row + 1):
            count = itertools.count(mark_out + n * which)
            copies = list(put_result(which, i))
            pl.when(row == i)(functools.partial(begin, *copies))
        return copies

    def on_row(i, *copies, act):
        pl.when(row == i)(functools.partial(act, *copies))

    for j in range(chans // 128):
        sh[j, 0:8, :] = jnp.zeros((8, 128), jnp.float32)
        sh[j, 8 + frames :, :] = jnp.zeros((8, 128), jnp.float32)

    inv_count = inv_ref[0]
    style = style_ref[0].astype(jnp.float32)
    finish_copies(*get_fr)
    on_row(0, get_tail, act=finish_copies)
    biases = w_ref[bias_at : bias_at + BLOCK, :].astype(jnp.float32)

    def project(layer, k):
        proj = jnp.dot(
            style, w_ref[fc_rows(layer, k), :].astype(jnp.float32),
            precision=highest, preferred_element_type=jnp.float32,
        )
        return proj + biases[2 * layer + k : 2 * layer + k + 1]

    def hold(b, v):
        at = pl.ds(pl.multiple_of(b * BLOCK + 8, 8), BLOCK)
        v = flat(v)
        for j in range(chans // 128):
            sh[j, at, :] = v[:, j * 128 : (j + 1) * 128]

    def statistics(src, layer):
        base = layer * 6
        acc[0] = jnp.zeros_like(acc[0])

        def add_values(b):
            v = keep(b, load(src, b))
            acc[0, segment(b)] += v[0] + v[1]

        loop(add_values)
        put(base, total(0) * inv_count)
        acc[0] = jnp.zeros_like(acc[0])

        def add_squares(b):
            s = segment(b)
            c = keep(b, load(src, b) - coef[base, s])
            c = c * c
            acc[0, s] += c[0] + c[1]

        loop(add_squares)
        var = total(0) * inv_count
        rstd = lax.rsqrt(jnp.maximum(var, var_floor))
        put(base + 1, (1.0 + project(layer, 0)) * rstd)
        put(base + 2, project(layer, 1))
        put(base + 3, rstd)
        put(base + 4, jnp.where(var > var_floor, rstd, 0.0) * inv_count)

    def activation(src, layer):
        base = layer * 6

        def body(b):
            s = segment(b)
            u = coef[base + 1, s] * (load(src, b) - coef[base, s]) + coef[base + 2, s]
            hold(b, keep(b, u * (0.5 * jnp.tanh(0.5 * u) + 0.5)))

        loop(body)

    def spread(dst, first):
        last = 2 - first

        def body(b):
            s = segment(b)
            from_row = jnp.where(seg_ref[row, b] == s, 0, 1)
            to_row = jnp.where(seg_ref[row, b + 2] == s, 8, 7)
            for j in range(chans // 128):

                def part(off):
                    return sh[j, pl.ds(b * BLOCK + off, 8), :]

                def store(tap, low, high):
                    at = tap * chans + j * 128
                    v = jnp.concatenate([low, high], axis=0)
                    dst[span(b), at : at + 128] = v.astype(dst.dtype)

                store(first, jnp.where(edge >= from_row, part(7), 0.0), part(15))
                store(1, part(8), part(16))
                store(last, part(9), jnp.where(edge < to_row, part(17), 0.0))

        loop(body)

    tile = min(frames, 1024)

    def convolve(dst, src, layer):
        def body(i, carry):
            at = pl.ds(pl.multiple_of(i * tile, tile), tile)
            dst[at, :] = jnp.dot(
                src[at, :], w_ref[layer * wide : (layer + 1) * wide, :],
                preferred_element_type=jnp.float32,
            )
            return carry

        lax.fori_loop(0, frames // tile, body, 0)

    def input_grad(dst, src, layer):
        def body(i, carry):
            at = pl.ds(pl.multiple_of(i * tile, tile), tile)
            dst[at, :] = lax.dot_general(
                src[at, :], wt_ref[layer], NT, preferred_element_type=jnp.float32
            )
            return carry

        lax.fori_loop(0, frames // tile, body, 0)

    def weight_grad(layer, kept, grads):
        def body(i, carry):
            at = pl.ds(pl.multiple_of(i * 256, 256), 256)
            to = pl.ds(pl.multiple_of(layer * wide + i * 256, 256), 256)
            sum_ref[to, :] += lax.dot_general(
                kept[:, at], grads[:, chans : 2 * chans], TN, preferred_element_type=jnp.float32
            )
            return carry

        lax.fori_loop(0, wide // 256, body, 0)

    def backward(src, layer):
        base = layer * 6
        acc[...] = jnp.zeros_like(acc)

        def body(b):
            s = segment(b)
            c = load(src, b) - coef[base, s]
            u = coef[base + 1, s] * c + coef[base + 2, s]
            sig = 0.5 * jnp.tanh(0.5 * u) + 0.5
            du = keep(b, load(da, b) * (sig * (1.0 + u * (1.0 - sig))))
            da[span(b), :] = flat(du)
            acc[0, s] += du[0] + du[1]
            duc = du * c
            acc[1, s] += duc[0] + duc[1]

        loop(body)
        dbeta = total(0)
        dgain = total(1) * coef[base + 3, :, 0, :]
        put(base + 4, coef[base + 4, :, 0, :] * dgain)
        put(base + 5, inv_count * dbeta)
        for k, d in enumerate((dgain, dbeta)):
            at = fc_rows(layer, k)
            sum_ref[at, :] += lax.dot_general(
                style, d, TN, precision=highest, preferred_element_type=jnp.float32
            )
            dstyle_ref[0] += lax.dot_general(
                d, w_ref[at, :].astype(jnp.float32), NT,
                precision=highest, preferred_element_type=jnp.float32,
            )
        return [jnp.sum(dgain, axis=0, keepdims=True), jnp.sum(dbeta, axis=0, keepdims=True)]

    def value_grad(src, layer, b):
        base = layer * 6
        s = segment(b)
        c = load(src, b) - coef[base, s]
        dv = coef[base + 1, s] * (load(da, b) - (c * coef[base + 4, s] + coef[base + 5, s]))
        return keep(b, dv)

    statistics(fr, 0)
    activation(fr, 0)
    spread(a3x, 0)
    on_row(0, *get_w[0], act=finish_copies)
    convolve(conv, a3x, 0)
    statistics(conv, 1)
    activation(conv, 1)
    spread(a3y, 0)
    on_row(0, *get_w[1], act=finish_copies)
    finish_copies(*get_ct)
    convolve(da, a3y, 1)
    bias = biases[4:5]
    acc[0, 0] = jnp.zeros_like(acc[0, 0])

    def finish(b):
        y = keep(b, load(da, b) + bias[None])
        res[span(b), :] = flat((load(fr, b) + y) * inv_root).astype(res.dtype)
        g = keep(b, load(ct, b) * inv_root).astype(jnp.bfloat16).astype(jnp.float32)
        hold(b, g)
        acc[0, 0] += g[0] + g[1]

    loop(finish)
    bias_sum = jnp.sum(acc[0, 0], axis=0, keepdims=True)
    put_output = start_result(0)

    dstyle_ref[...] = jnp.zeros_like(dstyle_ref)
    spread(g3, 2)
    on_row(0, *get_sums, act=finish_copies)
    weight_grad(1, a3y, g3)
    on_row(last_row, 1, act=send_sums)
    input_grad(da, g3, 1)
    rows_two = backward(conv, 1)

    def round_grad(b):
        hold(b, value_grad(conv, 1, b).astype(jnp.bfloat16).astype(jnp.float32))

    loop(round_grad)
    spread(g3, 2)
    weight_grad(0, a3x, g3)
    on_row(last_row, 0, act=send_sums)
    input_grad(da, g3, 0)
    rows_one = backward(fr, 0)

    sum_ref[bias_at : bias_at + 8, :] += jnp.concatenate(
        rows_one + rows_two + [bias_sum, jnp.zeros((3, chans), jnp.float32)], axis=0
    )
    on_row(last_row, 2, act=send_sums)
    finish_copies(*put_output)

    def frames_grad(b):
        dv = value_grad(fr, 0, b)
        res[span(b), :] = flat(load(ct, b) * inv_root + dv).astype(res.dtype)

    loop(frames_grad)
    finish_copies(*start_result(1))
    on_row(last_row, *put_sums, act=finish_copies)


def block_rows(
    n, per, first, z, lengths, seg_blocks, frames, cotangent, style, inv, weights,
    recv, from_f, from_c, to, prev, final,
):
    frames_n, width = frames.shape[1:]
    chans = width * n
    segs, style_n = style.shape[1:]
    flat_n = weights.shape[0]
    rows = len(to)
    f32 = jnp.float32

    def here(r, *_):
        return (first + r, 0, 0)

    received = [v for group in recv for v in group]
    any_space = pl.BlockSpec(memory_space=pl.ANY)
    in_specs = (
        [any_space] * 2
        + [pl.BlockSpec((1, segs, style_n), here), pl.BlockSpec((1, segs, chans), here)]
        + [any_space] * (1 + len(received) + len(prev))
    )
    out_shape = [
        jax.ShapeDtypeStruct((flat_n, chans), jnp.bfloat16 if final else f32),
        jax.ShapeDtypeStruct((rows, segs, style_n), f32),
    ]
    out_shape += [jax.ShapeDtypeStruct(frames.shape, jnp.bfloat16)] * 2
    for i in range(1 + max(i for i, _ in to)):
        size = 2 * sum(j == i for j, _ in to)
        out_shape += [jax.ShapeDtypeStruct((size, frames_n, width), jnp.bfloat16)] * (n - 1)
    out_specs = [any_space] * len(out_shape)
    out_specs[1] = pl.BlockSpec((1, segs, style_n), lambda r, *_: (r, 0, 0))
    scratch = [
        pltpu.VMEM((frames_n, chans), jnp.bfloat16),
        pltpu.VMEM((frames_n, chans), jnp.bfloat16),
        pltpu.VMEM((frames_n, chans), jnp.bfloat16),
        pltpu.VMEM((chans // 128, frames_n + 16, 128), f32),
        pltpu.VMEM((frames_n, 3 * chans), jnp.bfloat16),
        pltpu.VMEM((frames_n, 3 * chans), jnp.bfloat16),
        pltpu.VMEM((frames_n, 3 * chans), jnp.bfloat16),
        pltpu.VMEM((frames_n, chans), f32),
        pltpu.VMEM((frames_n, chans), f32),
        pltpu.VMEM((2, segs, 8, chans), f32),
        pltpu.VMEM((12, segs, 8, chans), f32),
        pltpu.VMEM((flat_n, chans), jnp.bfloat16),
        pltpu.VMEM((2, chans, 3 * chans), jnp.bfloat16),
        pltpu.VMEM((flat_n, chans), f32),
        pltpu.VMEM((flat_n if final else 16, chans), jnp.bfloat16),
        pltpu.SemaphoreType.DMA((4 * n + 16,)),
    ]
    first_prev = 3 + 5 + len(received)
    return pl.pallas_call(
        functools.partial(
            rows_kernel, n, segs, style_n, per, first, from_f, from_c, to, len(prev), final,
        ),
        grid_spec=pltpu.PrefetchScalarGridSpec(
            num_scalar_prefetch=3,
            grid=(rows,),
            in_specs=in_specs,
            out_specs=out_specs,
            scratch_shapes=scratch,
        ),
        out_shape=out_shape,
        input_output_aliases={first_prev + i: 1 + i for i in range(1, len(prev))},
        compiler_params=pltpu.CompilerParams(vmem_limit_bytes=48 << 20),
        cost_estimate=pl.CostEstimate(
            flops=int(COST * rows * 6 * 2 * 3 * frames_n * chans * chans), bytes_accessed=1000000,
            transcendentals=0,
        ),
    )(
        z, lengths, seg_blocks, frames, cotangent, style, inv, weights,
        *received, *prev,
    )


def pack_kernel(n, per, part, z_ref, i_ref, frames, conv1, conv2, fc1, fc2, biases, *refs):
    outs, mine = refs[: n - 1], refs[n - 1]
    stage, rows, sems = refs[n:]
    count = itertools.count()

    def copy(src, dst):
        c = pltpu.make_async_copy(src, dst, sems.at[next(count)])
        c.start()
        return c

    frames_n = frames.shape[1]
    at, staged = 0, []
    for ref in (conv1, conv2, fc1, fc2, biases):
        staged.append(copy(ref, stage.at[pl.ds(at, ref.shape[0]), :]))
        at += ref.shape[0]
    read = []
    for k in range(1, n):
        read.append(copy(frames.at[lax.rem(z_ref[0] + k, n) * per], rows.at[k - 1]))
    sent = []
    if at < stage.shape[0]:
        stage[at:, :] = jnp.zeros((stage.shape[0] - at, stage.shape[1]), stage.dtype)
    for c in staged:
        c.wait()
    src = stage.at[pl.ds(pl.multiple_of(i_ref[0] * part, 16), part), :]
    sent.append(copy(src, mine))
    for k in range(1, n):
        sent.append(copy(src, outs[k - 1].at[pl.ds(frames_n, part), :]))
        read[k - 1].wait()
        sent.append(copy(rows.at[k - 1], outs[k - 1].at[pl.ds(0, frames_n), :]))
    for c in sent:
        c.wait()


def pack(n, n_rows, per, z, i, frames, weights):
    frames_n, width = frames.shape[1:]
    rows = sum(v.shape[0] for v in weights)
    padded = -(-rows // (16 * n_rows)) * 16 * n_rows
    part = padded // n_rows
    any_space = pl.BlockSpec(memory_space=pl.ANY)
    return pl.pallas_call(
        functools.partial(pack_kernel, n, per, part),
        grid_spec=pltpu.PrefetchScalarGridSpec(
            num_scalar_prefetch=2,
            grid=(1,),
            in_specs=[any_space] * (1 + len(weights)),
            out_specs=[any_space] * n,
            scratch_shapes=[
                pltpu.VMEM((padded, width), jnp.bfloat16),
                pltpu.VMEM((n - 1, frames_n, width), jnp.bfloat16),
                pltpu.SemaphoreType.DMA((3 * n + len(weights),)),
            ],
        ),
        out_shape=[jax.ShapeDtypeStruct((frames_n + part, width), jnp.bfloat16)] * (n - 1)
        + [jax.ShapeDtypeStruct((part, width), jnp.bfloat16)],
        compiler_params=pltpu.CompilerParams(vmem_limit_bytes=56 << 20),
        cost_estimate=pl.CostEstimate(flops=0, bytes_accessed=6 * padded * width, transcendentals=0),
    )(z, i, frames, *weights)


def bundle_kernel(n, per, names, z_ref, frames, cotangent, *refs):
    outs, stage, sems = refs[: n - 1], refs[n - 1], refs[n]
    frames_n = frames.shape[1]
    count = itertools.count()

    def copy(src, dst):
        c = pltpu.make_async_copy(src, dst, sems.at[next(count)])
        c.start()
        return c

    read = []
    for k in range(1, n):
        for i, (v, r) in enumerate(names):
            src = (frames if v == "f" else cotangent).at[lax.rem(z_ref[0] + k, n) * per + r]
            at = pl.ds(i * frames_n, frames_n)
            read.append((k, at, copy(src, stage.at[k - 1, at, :])))
    sent = []
    for k, at, c in read:
        c.wait()
        sent.append(copy(stage.at[k - 1, at, :], outs[k - 1].at[at, :]))
    for c in sent:
        c.wait()


def bundle_rows(n, per, names, z, frames, cotangent):
    frames_n, width = frames.shape[1:]
    size = len(names) * frames_n
    any_space = pl.BlockSpec(memory_space=pl.ANY)
    return pl.pallas_call(
        functools.partial(bundle_kernel, n, per, names),
        grid_spec=pltpu.PrefetchScalarGridSpec(
            num_scalar_prefetch=1,
            grid=(1,),
            in_specs=[any_space] * 2,
            out_specs=[any_space] * (n - 1),
            scratch_shapes=[
                pltpu.VMEM((n - 1, size, width), jnp.bfloat16),
                pltpu.SemaphoreType.DMA((2 * (n - 1) * len(names),)),
            ],
        ),
        out_shape=[jax.ShapeDtypeStruct((size, width), jnp.bfloat16)] * (n - 1),
        compiler_params=pltpu.CompilerParams(vmem_limit_bytes=56 << 20),
        cost_estimate=pl.CostEstimate(
            flops=0, bytes_accessed=4 * (n - 1) * size * width, transcendentals=0
        ),
    )(z, frames, cotangent)


def place_kernel(n, row, z_ref, *refs):
    pieces, refs = refs[: n - 1], refs[n - 1 :]
    results, stage, sems = refs[2:4], refs[4], refs[5]
    read = [
        pltpu.make_async_copy(ref, stage.at[k], sems.at[0, k]) for k, ref in enumerate(pieces)
    ]
    for c in read:
        c.start()
    sent = []
    for k, c in enumerate(read):
        c.wait()
        for which in range(2):
            dst = results[which].at[lax.rem(z_ref[0] + k + 1, n), row]
            sent.append(pltpu.make_async_copy(stage.at[k, which], dst, sems.at[1 + which, k]))
            sent[-1].start()
    for c in sent:
        c.wait()


def place(n, row, z, pieces, results):
    any_space = pl.BlockSpec(memory_space=pl.ANY)
    return pl.pallas_call(
        functools.partial(place_kernel, n, row),
        grid_spec=pltpu.PrefetchScalarGridSpec(
            num_scalar_prefetch=1,
            grid=(1,),
            in_specs=[any_space] * (n + 1),
            out_specs=[any_space] * 2,
            scratch_shapes=[
                pltpu.VMEM((n - 1,) + pieces[0].shape, jnp.bfloat16),
                pltpu.SemaphoreType.DMA((3, n - 1)),
            ],
        ),
        out_shape=[jax.ShapeDtypeStruct(v.shape, v.dtype) for v in results],
        input_output_aliases={n: 0, n + 1: 1},
        compiler_params=pltpu.CompilerParams(vmem_limit_bytes=56 << 20),
        cost_estimate=pl.CostEstimate(
            flops=0, bytes_accessed=4 * (n - 1) * pieces[0].size, transcendentals=0
        ),
    )(z, *pieces, *results)


def per_device(
    n,
    n_rows,
    frames,
    style_vector,
    segment_ids,
    padding,
    fc1_weight,
    fc1_bias,
    conv1_weight,
    fc2_weight,
    fc2_bias,
    conv2_weight,
    conv2_bias,
    cotangent,
):
    f32 = jnp.float32
    held, frames_n, width = frames.shape
    segs, style_n = style_vector.shape[1:]
    chans = n * width
    per = held // n
    z = lax.axis_index("ch")

    def shift(k):
        return [(i, (i + k) % n) for i in range(n)]

    def send(v, k, what):
        with jax.named_scope(what):
            return lax.ppermute(v, "ch", shift(k))

    def over_ch(v, pieces, axis):
        whole = jnp.concatenate([v] * n, axis=axis)
        size = v.shape[axis]
        for k, piece in enumerate(pieces, 1):
            at = lax.rem(z + n - k, n) * size
            whole = lax.dynamic_update_slice_in_dim(whole, piece, at, axis)
        return whole

    def after(v, others):
        return lax.optimization_barrier((v, others))[0]

    sizes = [3 * chans, 3 * chans, 2 * style_n, 2 * style_n, 2, 2, 1]
    used = sum(sizes)
    biases = jnp.concatenate(
        [fc1_bias, fc2_bias, conv2_bias[None], jnp.zeros((11, width), fc1_bias.dtype)]
    )
    shard = [v.reshape(-1, width) for v in (conv1_weight, conv2_weight, fc1_weight, fc2_weight)]
    *bundles, mine = pack(
        n, n_rows, per, z[None], lax.axis_index("rows")[None], frames, shard + [biases]
    )

    def piece(v, k, r):
        at = lax.rem(z + k, n) * per + r
        return lax.dynamic_slice_in_dim(v, at, 1, 0)[0]

    def swap(v, what):
        with jax.named_scope(what):
            return lax.all_to_all(v, "ch", 0, 0)

    def of_row(v, r):
        return v.reshape(n, per, frames_n, width)[:, r]

    def bundle(*names):
        return bundle_rows(n, per, names, z[None], frames, cotangent)

    def fetch(what, pieces):
        return [send(v, k, what) for k, v in enumerate(pieces, 1)]

    half = per // 2
    early = [(v, r) for r in range(half) for v in "fc"]
    late = [(v, r) for r in range(half, per) for v in "fc"]
    got_a = fetch("frames_0", bundles)
    got_b = fetch("inputs_1", bundle(*early[1:]))
    got_c = fetch("inputs_2", after(bundle(*late), got_b[1]))
    mine = over_ch(mine, [v[frames_n:] for v in got_a], 1)
    mine = after(mine, got_b[1])
    weights = lax.all_gather(mine, "rows", axis=0, tiled=True)

    first = z * per
    my_ids = lax.dynamic_slice_in_dim(segment_ids, first, per, 0)
    my_pad = lax.dynamic_slice_in_dim(padding, first, per, 0)
    my_style = lax.dynamic_slice_in_dim(style_vector, first, per, 0)
    lengths = jnp.sum(my_pad, axis=1).astype(jnp.int32)
    side = jnp.full((per, 1), -1, jnp.int32)
    seg_blocks = jnp.concatenate([side, my_ids[:, ::BLOCK], side], axis=1)
    counts = jnp.sum(
        jnp.where(my_ids[:, :, None] == jnp.arange(segs, dtype=jnp.int32), my_pad[:, :, None], 0),
        axis=1,
    ).astype(f32)
    inv_count = jnp.broadcast_to(
        (1.0 / jnp.maximum(counts, 1.0))[:, :, None], (per, segs, chans)
    )

    def run(first, count, recv, from_f, from_c, to, prev):
        ids, sizes = seg_blocks[first : first + count], lengths[first : first + count]
        return block_rows(
            n, per, first, z[None], sizes, ids, frames, cotangent, my_style, inv_count, weights,
            recv, from_f, from_c, to, prev, bool(prev),
        )

    def spots(group, skip, which, rows):
        return [(group, (2 * r + which - skip) * frames_n) for r in rows]

    sums, dstyle_a, *rest = run(
        0, half, [got_a, got_b], [(0, 0)] + spots(1, 1, 0, range(1, half)),
        spots(1, 1, 1, range(half)), [(0, r) for r in range(half)], [],
    )
    own, pieces = rest[:2], after(rest[2:], got_c)
    back = [[send(v, n - k, "results_0") for k, v in enumerate(pieces, 1)]]
    others = range(per - half)
    sums, dstyle_b, *rest = run(
        half, per - half, [got_c], spots(0, 0, 0, others), spots(0, 0, 1, others),
        [(r, 0) for r in others], [sums, *own],
    )
    own, pieces = rest[:2], rest[2:]
    for r in others:
        group = pieces[r * (n - 1) : (r + 1) * (n - 1)]
        if r == 0:
            group = [group[0], *after(group[1:], back[0][2])]
        back.append([send(v, n - k, f"results_{half + r}") for k, v in enumerate(group, 1)])
    dstyles = [dstyle_a, dstyle_b]

    sums = after(sums, back[0][1:])
    sums = lax.psum_scatter(sums, "rows", scatter_dimension=0, tiled=True)
    sums = after(sums, [back[1][0], back[1][2]])
    style_grad = jnp.concatenate(dstyles, axis=0).reshape(per * segs, style_n).astype(sums.dtype)

    def share(k):
        at = lax.rem(z + k, n) * width
        return lax.dynamic_slice_in_dim(sums, at, width, 1)

    got = [send(jnp.concatenate([share(k), style_grad]), k, "sums") for k in range(1, n)]
    part = sums.shape[0]
    total = share(0).astype(f32)
    for v in got:
        total = total + v[:part].astype(f32)
    grad_style = over_ch(style_grad, [v[part:] for v in got], 0)
    grad_style = grad_style.astype(f32).reshape(style_vector.shape)
    total = after(total, [back[1][1]])
    grads = lax.all_gather(total, "rows", axis=0, tiled=True)
    splits = [sum(sizes[: i + 1]) for i in range(len(sizes))]
    g1, g2, gf1, gf2, gb1, gb2, gb = [
        grads[end - size : end] for size, end in zip(sizes, splits)
    ]
    grads = [
        gf1.reshape(fc1_weight.shape),
        gb1,
        g1.reshape(conv1_weight.shape),
        gf2.reshape(fc2_weight.shape),
        gb2,
        g2.reshape(conv2_weight.shape),
        gb[0],
    ]

    results = [v.reshape(n, per, frames_n, width) for v in own]
    for r in range(per):
        if r == per - 1:
            grads, results = lax.optimization_barrier((grads, results))
            results = place(n, r, z[None], back[-1], results)
            break
        group, at = (0, r) if r < half else (r - half + 1, 0)
        for which in range(2):
            for k, v in enumerate(back[group], 1):
                results[which] = lax.dynamic_update_slice(
                    results[which], v[None, None, 2 * at + which], (lax.rem(z + k, n), r, 0, 0)
                )
    output, grad_frames = [v.reshape(frames.shape) for v in results]
    return (output, grad_frames, grad_style, *grads)


def solution(mesh):
    return jax.shard_map(
        functools.partial(per_device, mesh.shape["ch"], mesh.shape["rows"]),
        mesh=mesh,
        in_specs=(
            P("rows", None, "ch"),
            P("rows", None, None),
            P("rows", None),
            P("rows", None),
            P(None, None, "ch"),
            P(None, "ch"),
            P(None, None, "ch"),
            P(None, None, "ch"),
            P(None, "ch"),
            P(None, None, "ch"),
            P("ch"),
            P("rows", None, "ch"),
        ),
        out_specs=(
            P("rows", None, "ch"),
            P("rows", None, "ch"),
            P("rows", None, None),
            P(None, None, "ch"),
            P(None, "ch"),
            P(None, None, "ch"),
            P(None, None, "ch"),
            P(None, "ch"),
            P(None, None, "ch"),
            P("ch"),
        ),
        check_vma=False,
    )
```
